32 devices in a mesh: kring: 16 (over z, x, core), slab: 2 (over y).
Axes of the slice: x: 2, y: 2, z: 4, core: 2. Of those that a mesh axis runs over, the one named last changes fastest.
Arguments:
- targets: float32 [16, 2, 2, 16, 256], P('kring', None, None, 'slab'), may hold values from -6 to 6
- orbitals: float32 [16, 32, 2, 16, 256], P('kring', None, None, 'slab'), may hold values from -6 to 6
- block_index: int32 [16], P('kring'), may hold values from 0 to 1
- occupied: int32 [16, 32], P('kring'), may hold values 0 or 1
- kpoint: int32 [16], replicated, may hold values from 0 to 15, each once
Outputs:
- exchange: float32 [16, 2, 2, 16, 256], P('kring', None, None, 'slab')
- projection: float32 [16, 2, 2, 2], P('kring')
The draws below stay inside these ranges and needn't reach their ends.
Inputs may be any that keep to these rules, and one draw needn't show every extreme that they name: `kpoint`: every label appears at exactly one cycle position.
All inputs are finite; a program needn't handle non-finite values. No bound on the sum of `occupied` on one device may be relied on, other than what follows from the above.
Results may differ from the reference program's by a relative error of at most 0.0003.
Values sent between devices are 32-bit elements; how exact they have to be, the bound alone decides.
No kernel may reach another device: no remote copies, remote signals or barrier semaphores. Data moves between devices by JAX's collectives and lax.ppermute only.
A program may use at most 64 MiB of HBM per device.

```python
import math
import jax
import jax.numpy as jnp
from jax import lax

CX = 2
CY = 128
TARGETS = 2
BLOCKS = 2
BLOCK = 16
HALF = 2
NK = 16
NZ = 16


def set_ends(entries, rng, low, top_value):
    spot = [jax.random.randint(jax.random.fold_in(rng, axis), (), 0, length) for axis, length in enumerate(entries.shape)]
    main_axis = entries.shape.index(max(entries.shape))
    beside = spot[:main_axis] + [(spot[main_axis] + 1) % entries.shape[main_axis]] + spot[main_axis + 1:]
    return entries.at[tuple(spot)].set(low).at[tuple(beside)].set(top_value)


def shard_levels(stream_key, shape, cuts, least, top_value):
    def one(position, blocks):
        steps = jax.random.uniform(jax.random.fold_in(jax.random.fold_in(stream_key, 6), position), (blocks,), jnp.float32, least / len(cuts), top_value / len(cuts))
        return jnp.repeat(jnp.exp(steps), shape[position] // blocks).reshape((-1,) + (1,) * (len(shape) - position - 1))

    loudness = one(*cuts[0])
    for cut in cuts[1:]:
        loudness = loudness * one(*cut)
    return loudness


def scatter_about(own_key, extent, spread, reach, cuts=(), kind=jnp.bfloat16):
    drawn = jax.random.normal(own_key, extent, jnp.float32) * spread
    if len(cuts) > 0:
        drawn = shard_levels(own_key, extent, cuts, -0.22, 0.18) * drawn
    return jnp.clip(drawn, min=-reach, max=reach).astype(kind)


def setup_inputs(seed: int = 0) -> dict:
    seeds = jax.random.split(jax.random.key(seed), 6)
    targets = scatter_about(seeds[0], (NK, TARGETS, 2, NZ, CX * CY), 1.0, 6.0, ((0, 16), (3, 2)), jnp.float32)
    orbitals = scatter_about(seeds[1], (NK, BLOCKS * BLOCK, 2, NZ, CX * CY), 1.0, 6.0, ((0, 16), (3, 2)), jnp.float32)
    block_index = set_ends(jax.random.randint(seeds[2], (NK,), 0, BLOCKS), jax.random.fold_in(seeds[2], 1), 0, BLOCKS - 1).astype(jnp.int32)
    occupied = set_ends((jax.random.randint(seeds[3], (NK, BLOCKS * BLOCK), 0, 4) < 3).astype(jnp.int32), jax.random.fold_in(seeds[3], 1), 0, 1)
    kpoint = jax.random.permutation(seeds[4], NK).astype(jnp.int32)
    return dict(targets=targets, orbitals=orbitals, block_index=block_index, occupied=occupied, kpoint=kpoint)


DIAG = 7.0


def pair_density(psi, phi):
    psi_re = psi[:, None, 0]
    psi_im = psi[:, None, 1]
    phi_re = phi[None, :, 0]
    phi_im = phi[None, :, 1]
    rho_re = phi_re * psi_re + phi_im * psi_im
    rho_im = phi_re * psi_im - phi_im * psi_re
    return jnp.stack([rho_re, rho_im], axis=2)


def plane_sum(field):
    cells = field.shape[-1]
    column = jnp.mod(jnp.arange(cells, dtype=jnp.int32), CY)
    below_y = jnp.where(column == 0, jnp.roll(field, -(CY - 1), -1), jnp.roll(field, 1, -1))
    above_y = jnp.where(column == CY - 1, jnp.roll(field, CY - 1, -1), jnp.roll(field, -1, -1))
    below_x = jnp.roll(field, CY, -1)
    above_x = jnp.roll(field, -CY, -1)
    return below_y + above_y + below_x + above_x


def contribution(psi, phi, theta):
    cosine = jnp.cos(theta)
    sine = jnp.sin(theta)
    rho = pair_density(psi, phi)
    first = rho / DIAG
    upper = jnp.roll(first, -1, axis=3)
    lower = jnp.roll(first, 1, axis=3)
    plane = plane_sum(first)
    near_re = plane[:, :, 0] + cosine * (upper[:, :, 0] + lower[:, :, 0]) - sine * (upper[:, :, 1] - lower[:, :, 1])
    near_im = plane[:, :, 1] + cosine * (upper[:, :, 1] + lower[:, :, 1]) + sine * (upper[:, :, 0] - lower[:, :, 0])
    second = (rho + jnp.stack([near_re, near_im], axis=2)) / DIAG
    phi_re = phi[None, :, 0]
    phi_im = phi[None, :, 1]
    out_re = -jnp.sum(second[:, :, 0] * phi_re - second[:, :, 1] * phi_im, axis=1)
    out_im = -jnp.sum(second[:, :, 0] * phi_im + second[:, :, 1] * phi_re, axis=1)
    return jnp.stack([out_re, out_im], axis=1)


def pick_block(orb, first_band, occ):
    block = lax.dynamic_slice_in_dim(orb, first_band, BLOCK, 0)
    weight = lax.dynamic_slice_in_dim(occ, first_band, BLOCK, 0).astype(jnp.float32)
    return block * weight[:, None, None, None]


def reference(targets, orbitals, block_index, occupied, kpoint):
    starts = (block_index * BLOCK).astype(jnp.int32)
    blocks = jax.vmap(pick_block)(orbitals, starts, occupied)

    def one_point(place):
        psi = targets[place]
        total = jnp.zeros(psi.shape, jnp.float32)
        for offset in range(-HALF, HALF + 1):
            source = jnp.mod(place + offset, NK).astype(jnp.int32)
            theta = (kpoint[place] - kpoint[source]).astype(jnp.float32) * (2.0 * math.pi / NK)
            total = total + contribution(psi, blocks[source], theta)
        flat_psi = psi.reshape(psi.shape[0], 2, -1)
        flat_out = total.reshape(total.shape[0], 2, -1)
        real_part = jnp.einsum("apc,bpc->ab", flat_psi, flat_out, precision=lax.Precision.HIGHEST)
        imag_part = jnp.einsum("ac,bc->ab", flat_psi[:, 0], flat_out[:, 1], precision=lax.Precision.HIGHEST) - jnp.einsum("ac,bc->ab", flat_psi[:, 1], flat_out[:, 0], precision=lax.Precision.HIGHEST)
        tile = jnp.stack([real_part, imag_part], axis=-1) / (NZ * CX * CY)
        return total, tile

    exchange, projection = lax.map(one_point, jnp.arange(NK, dtype=jnp.int32))
    return exchange, projection
```

```python
import math

import jax
import jax.numpy as jnp
from jax import lax
from jax.experimental import pallas as pl
from jax.experimental.pallas import tpu as pltpu
from jax.sharding import PartitionSpec as P

CX = 2
CY = 128
CELLS = CX * CY
BLOCK = 16
FIELDS = 6
DIAG = 7.0

VMEM = pl.BlockSpec(memory_space=pltpu.VMEM)
SMEM = pl.BlockSpec(memory_space=pltpu.SMEM)
ANY = pl.BlockSpec(memory_space=pl.ANY)


def halves(field):
    return field[:, :CY], field[:, CY:]


def turn(field, shift):
    a, b = halves(field)
    amount = (-shift) % CY
    return jnp.concatenate([pltpu.roll(a, amount, 1), pltpu.roll(b, amount, 1)], axis=1)


def swap_x(field):
    a, b = halves(field)
    return jnp.concatenate([b, a], axis=1)


def bond(ar, ai, br, bi):
    return ar * br + ai * bi, ai * br - ar * bi


def gather_kernel(planes, index_ref, occupied_ref, psi_hbm, orb_hbm, pack_ref, orb, sems):
    rows = 2 * planes
    field_rows = FIELDS * planes
    end_rows = 4 * BLOCK
    psi_rows = psi_hbm.shape[0]
    loads = [pltpu.make_async_copy(orb_hbm.at[:, pl.ds(x * CY, CY)], orb.at[x], sems.at[x]) for x in range(CX)]
    for load in loads:
        load.start()
    keep = pltpu.make_async_copy(psi_hbm, pack_ref.at[pl.ds(field_rows + end_rows, psi_rows)], sems.at[CX])
    keep.start()
    first = index_ref[0] * BLOCK
    weights = [occupied_ref[0, first + m].astype(jnp.float32) for m in range(BLOCK)]
    for load in loads:
        load.wait()
    dens = jnp.zeros((planes, CELLS), jnp.float32)
    dx_re = jnp.zeros((planes, CY), jnp.float32)
    dx_im = jnp.zeros((planes, CY), jnp.float32)
    dy_re, dy_im, dz_re, dz_im = dens, dens, dens, dens
    for m in range(BLOCK):
        base = pl.multiple_of((first + m) * rows, 8)
        re = jnp.concatenate([orb[x, pl.ds(base, planes), :] for x in range(CX)], axis=1) * weights[m]
        im = jnp.concatenate([orb[x, pl.ds(base + planes, planes), :] for x in range(CX)], axis=1) * weights[m]
        dens = dens + re * re + im * im
        re0, re1 = halves(re)
        im0, im1 = halves(im)
        part = bond(re0, im0, re1, im1)
        dx_re, dx_im = dx_re + part[0], dx_im + part[1]
        part = bond(re, im, turn(re, 1), turn(im, 1))
        dy_re, dy_im = dy_re + part[0], dy_im + part[1]
        part = bond(re, im, pltpu.roll(re, planes - 1, 0), pltpu.roll(im, planes - 1, 0))
        dz_re, dz_im = dz_re + part[0], dz_im + part[1]
    for i, field in enumerate((dens, jnp.concatenate([dx_re, dx_im], axis=1), dy_re, dy_im, dz_re, dz_im)):
        pack_ref[pl.ds(i * planes, planes), :] = field
    band = lax.broadcasted_iota(jnp.int32, (BLOCK, 1), 0)
    column = jnp.zeros((BLOCK, 1), jnp.float32)
    for m in range(BLOCK):
        column = jnp.where(band == m, weights[m], column)
    for e, plane in enumerate((0, planes - 1)):
        for c in range(2):
            start = first * rows + c * planes + plane
            for x in range(CX):
                ends = orb[x, pl.ds(start, BLOCK, stride=rows), :] * column
                pack_ref[pl.ds(field_rows + (2 * e + c) * BLOCK, BLOCK), pl.ds(x * CY, CY)] = ends
    keep.wait()


def gather(block_index, occupied, psi, orb, planes):
    psi_rows = psi.shape[0]
    total = FIELDS * planes + 4 * BLOCK + psi_rows

    def body(*refs):
        gather_kernel(planes, *refs)

    return pl.pallas_call(
        body,
        out_shape=jax.ShapeDtypeStruct((total, CELLS), jnp.float32),
        in_specs=[SMEM, SMEM, ANY, ANY],
        out_specs=VMEM,
        scratch_shapes=[pltpu.VMEM((CX, orb.shape[0], CY), jnp.float32), pltpu.SemaphoreType.DMA((CX + 1,))],
        name="local_fields",
    )(block_index, occupied, psi, orb)


def join(phase, packs, planes):
    count = len(packs)
    field_rows = FIELDS * planes

    def body(phase_ref, *refs):
        ins, out = refs[:count], refs[count]
        cosine, sine = phase_ref[0], phase_ref[1]
        last = lax.broadcasted_iota(jnp.int32, (planes, CELLS), 0) == planes - 1

        def end(ref, e, c):
            return ref[pl.ds(field_rows + (2 * e + c) * BLOCK, BLOCK), :]

        for d in range(count):
            here, there = ins[d], ins[(d + 1) % count]
            out[pl.ds(d * field_rows, 4 * planes), :] = here[pl.ds(0, 4 * planes), :]
            re, im = bond(end(here, 1, 0), end(here, 1, 1), end(there, 0, 0), end(there, 0, 1))
            re = jnp.sum(re, axis=0, keepdims=True)
            im = jnp.sum(im, axis=0, keepdims=True)
            re = jnp.where(last, re, here[pl.ds(4 * planes, planes), :])
            im = jnp.where(last, im, here[pl.ds(5 * planes, planes), :])
            out[pl.ds(d * field_rows + 4 * planes, planes), :] = re * cosine + im * sine
            out[pl.ds(d * field_rows + 5 * planes, planes), :] = im * cosine - re * sine

    return pl.pallas_call(
        body,
        out_shape=jax.ShapeDtypeStruct((count * field_rows, CELLS), jnp.float32),
        in_specs=[SMEM] + [VMEM] * count,
        out_specs=VMEM,
        name="join_slabs",
    )(phase, *packs)


def apply(phase, parts, packs, planes, bands):
    count = len(packs)
    field_rows = FIELDS * planes
    psi_start = field_rows + 4 * BLOCK
    scale = 1.0 / (count * planes * CELLS)

    def body(phase_ref, *refs):
        part_refs, ins = refs[: len(parts)], refs[len(parts) : len(parts) + count]
        out_ref, tile_ref = refs[len(parts) + count :]
        cosine, sine = phase_ref[0], phase_ref[1]
        row = lax.broadcasted_iota(jnp.int32, (planes, CELLS), 0)

        def window(d, i, offset=0):
            at = pl.ds(d * field_rows + i * planes, planes)
            total = part_refs[0][at, :]
            for ref in part_refs[1:]:
                total = total + ref[at, :]
            return total

        def psi_at(d, b, c):
            return ins[d % count][pl.ds(psi_start + (2 * b + c) * planes, planes), :]

        def above(d, field):
            return jnp.where(row == planes - 1, pltpu.roll(field(d + 1), planes - 1, 0), pltpu.roll(field(d), planes - 1, 0))

        def below(d, field):
            return jnp.where(row == 0, pltpu.roll(field(d - 1), 1, 0), pltpu.roll(field(d), 1, 0))

        up = []
        for d in range(count):
            re, im = window(d, 4), window(d, 5)
            up.append((re * cosine - im * sine, im * cosine + re * sine))
        sums = [[[None, None] for _ in range(bands)] for _ in range(bands)]
        for d in range(count):
            dens = window(d, 0) * (1.0 / DIAG)
            dx_re, dx_im = halves(window(d, 1))
            x_re = jnp.concatenate([dx_re, dx_re], axis=1) * 2.0
            x_im = jnp.concatenate([dx_im, -dx_im], axis=1) * 2.0
            y_re, y_im = window(d, 2), window(d, 3)
            yb_re, yb_im = turn(y_re, -1), -turn(y_im, -1)
            z_re, z_im = up[d]
            zb_re = below(d, lambda e: up[e % count][0])
            zb_im = -below(d, lambda e: up[e % count][1])
            results = []
            for b in range(bands):
                re, im = psi_at(d, b, 0), psi_at(d, b, 1)
                acc_re = jnp.zeros_like(re)
                acc_im = jnp.zeros_like(re)
                terms = (
                    (x_re, x_im, swap_x(re), swap_x(im)),
                    (y_re, y_im, turn(re, 1), turn(im, 1)),
                    (yb_re, yb_im, turn(re, -1), turn(im, -1)),
                    (z_re, z_im, above(d, lambda e: psi_at(e, b, 0)), above(d, lambda e: psi_at(e, b, 1))),
                    (zb_re, zb_im, below(d, lambda e: psi_at(e, b, 0)), below(d, lambda e: psi_at(e, b, 1))),
                )
                for wr, wi, vr, vi in terms:
                    acc_re = acc_re + (wr * vr - wi * vi)
                    acc_im = acc_im + (wr * vi + wi * vr)
                out_re = -(dens * re + acc_re * (1.0 / (DIAG * DIAG)))
                out_im = -(dens * im + acc_im * (1.0 / (DIAG * DIAG)))
                results.append((out_re, out_im))
                if d == 0:
                    out_ref[pl.ds(2 * b * planes, planes), :] = out_re
                    out_ref[pl.ds((2 * b + 1) * planes, planes), :] = out_im
            for a in range(bands):
                re, im = psi_at(d, a, 0), psi_at(d, a, 1)
                for b in range(bands):
                    out_re, out_im = results[b]
                    both = (re * out_re + im * out_im, re * out_im - im * out_re)
                    for c in range(2):
                        old = sums[a][b][c]
                        sums[a][b][c] = both[c] if old is None else old + both[c]
        shape = (bands, 2)
        first = lax.broadcasted_iota(jnp.int32, shape, 0)
        second = lax.broadcasted_iota(jnp.int32, shape, 1)
        for a in range(bands):
            tile = jnp.zeros(shape, jnp.float32)
            for b in range(bands):
                for c in range(2):
                    folded = sums[a][b][c]
                    folded = folded[:, :CY] + folded[:, CY:]
                    value = jnp.sum(jnp.sum(folded, axis=0, keepdims=True), axis=1, keepdims=True)
                    tile = jnp.where((first == b) & (second == c), value * scale, tile)
            tile_ref[0, a] = tile

    return pl.pallas_call(
        body,
        out_shape=(
            jax.ShapeDtypeStruct((2 * bands * planes, CELLS), jnp.float32),
            jax.ShapeDtypeStruct((1, bands, bands, 2), jnp.float32),
        ),
        in_specs=[SMEM] + [VMEM] * (len(parts) + count),
        out_specs=(VMEM, VMEM),
        name="apply_window",
    )(phase, *parts, *packs)


def shift(value, axis, distance):
    count = lax.axis_size(axis)
    return lax.ppermute(value, axis, [((i + distance) % count, i) for i in range(count)])


def body(targets, orbitals, block_index, occupied, kpoint):
    bands, planes = targets.shape[1], targets.shape[3]
    cycle, slabs = lax.axis_size("kring"), lax.axis_size("slab")
    place = lax.axis_index("kring")
    psi = targets.reshape(2 * bands * planes, CELLS)
    orb = orbitals.reshape(-1, CELLS)

    angle = lax.dynamic_index_in_dim(kpoint, place, 0, False).astype(jnp.float32) * (2.0 * math.pi / cycle)
    phase = jnp.stack([jnp.cos(angle), jnp.sin(angle)])

    own = gather(block_index, occupied, psi, orb, planes)
    packs = [own] + [shift(own, "slab", d) for d in range(1, slabs)]
    mine = join(phase, packs, planes)

    other = lax.ppermute(mine, "kring", [(i, i ^ 1) for i in range(cycle)])
    pair = mine + other
    even = lax.rem(place, 2) == 0
    left = shift(jnp.where(even, pair, mine), "kring", -2)
    right = shift(jnp.where(even, mine, pair), "kring", 2)
    exchange, tile = apply(phase, [pair, left, right], packs, planes, bands)
    return exchange.reshape(targets.shape), tile


def solution(mesh):
    placed = (
        P("kring", None, None, "slab", None),
        P("kring", None, None, "slab", None),
        P("kring"),
        P("kring", None),
        P(),
    )
    return jax.shard_map(
        body,
        mesh=mesh,
        in_specs=placed,
        out_specs=(P("kring", None, None, "slab", None), P("kring", None, None, None)),
        check_vma=False,
    )
```

```python
import math

import jax
import jax.numpy as jnp
from jax import lax
from jax.experimental import pallas as pl
from jax.experimental.pallas import tpu as pltpu
from jax.sharding import PartitionSpec as P

CX = 2
CY = 128
CELLS = CX * CY
BLOCK = 16
FIELDS = 6
DIAG = 7.0

VMEM = pl.BlockSpec(memory_space=pltpu.VMEM)
SMEM = pl.BlockSpec(memory_space=pltpu.SMEM)
HBM = pl.BlockSpec(memory_space=pltpu.HBM)
PARAMS = pltpu.CompilerParams(vmem_limit_bytes=4 * 1024 * 1024)


def halves(field):
    return field[:, :CY], field[:, CY:]


def turn(field, shift):
    a, b = halves(field)
    amount = (-shift) % CY
    return jnp.concatenate([pltpu.roll(a, amount, 1), pltpu.roll(b, amount, 1)], axis=1)


def swap_x(field):
    a, b = halves(field)
    return jnp.concatenate([b, a], axis=1)


def bond(ar, ai, br, bi):
    return ar * br + ai * bi, ai * br - ar * bi


def gather_kernel(planes, index_ref, occupied_hbm, psi_hbm, orb_hbm, pack_ref, orb, occupied_ref, sems):
    rows = 2 * planes
    field_rows = FIELDS * planes
    end_rows = 4 * BLOCK
    psi_rows = psi_hbm.shape[0]
    loads = [pltpu.make_async_copy(orb_hbm.at[:, pl.ds(x * CY, CY)], orb.at[x], sems.at[x]) for x in range(CX)]
    for load in loads:
        load.start()
    keep = pltpu.make_async_copy(psi_hbm, pack_ref.at[pl.ds(field_rows + end_rows, psi_rows)], sems.at[CX])
    keep.start()
    masks = pltpu.make_async_copy(occupied_hbm, occupied_ref, sems.at[CX + 1])
    masks.start()
    masks.wait()
    first = index_ref[0] * BLOCK
    weights = [occupied_ref[0, first + m].astype(jnp.float32) for m in range(BLOCK)]
    for load in loads:
        load.wait()
    dens = jnp.zeros((planes, CELLS), jnp.float32)
    dx_re = jnp.zeros((planes, CY), jnp.float32)
    dx_im = jnp.zeros((planes, CY), jnp.float32)
    dy_re, dy_im, dz_re, dz_im = dens, dens, dens, dens
    for m in range(BLOCK):
        base = pl.multiple_of((first + m) * rows, 8)
        re = jnp.concatenate([orb[x, pl.ds(base, planes), :] for x in range(CX)], axis=1) * weights[m]
        im = jnp.concatenate([orb[x, pl.ds(base + planes, planes), :] for x in range(CX)], axis=1) * weights[m]
        dens = dens + re * re + im * im
        re0, re1 = halves(re)
        im0, im1 = halves(im)
        part = bond(re0, im0, re1, im1)
        dx_re, dx_im = dx_re + part[0], dx_im + part[1]
        part = bond(re, im, turn(re, 1), turn(im, 1))
        dy_re, dy_im = dy_re + part[0], dy_im + part[1]
        part = bond(re, im, pltpu.roll(re, planes - 1, 0), pltpu.roll(im, planes - 1, 0))
        dz_re, dz_im = dz_re + part[0], dz_im + part[1]
    for i, field in enumerate((dens, jnp.concatenate([dx_re, dx_im], axis=1), dy_re, dy_im, dz_re, dz_im)):
        pack_ref[pl.ds(i * planes, planes), :] = field
    band = lax.broadcasted_iota(jnp.int32, (BLOCK, 1), 0)
    column = jnp.zeros((BLOCK, 1), jnp.float32)
    for m in range(BLOCK):
        column = jnp.where(band == m, weights[m], column)
    for e, plane in enumerate((0, planes - 1)):
        for c in range(2):
            start = first * rows + c * planes + plane
            for x in range(CX):
                ends = orb[x, pl.ds(start, BLOCK, stride=rows), :] * column
                pack_ref[pl.ds(field_rows + (2 * e + c) * BLOCK, BLOCK), pl.ds(x * CY, CY)] = ends
    keep.wait()


def phase_of(kpoint, place, cycle):
    def body(place_ref, kpoint_hbm, out_ref, labels, sem):
        load = pltpu.make_async_copy(kpoint_hbm, labels, sem)
        load.start()
        load.wait()
        label = labels[place_ref[0]].astype(jnp.float32)
        angle = jnp.full((8, CY), label * (2.0 * math.pi / cycle), jnp.float32)
        out_ref[pl.ds(0, 8), :] = jnp.cos(angle)
        out_ref[pl.ds(8, 8), :] = jnp.sin(angle)

    return pl.pallas_call(
        body,
        out_shape=jax.ShapeDtypeStruct((16, CY), jnp.float32),
        in_specs=[SMEM, HBM],
        out_specs=VMEM,
        scratch_shapes=[pltpu.SMEM(kpoint.shape, jnp.int32), pltpu.SemaphoreType.DMA],
        compiler_params=PARAMS,
        name="phase",
    )(place.reshape(1), kpoint)


def phase_rows(ref):
    return [jnp.concatenate([ref[pl.ds(8 * i, 1), :]] * CX, axis=1) for i in range(2)]


def gather(block_index, occupied, psi, orb, planes):
    psi_rows = psi.shape[0]
    total = FIELDS * planes + 4 * BLOCK + psi_rows

    def body(*refs):
        gather_kernel(planes, *refs)

    return pl.pallas_call(
        body,
        out_shape=jax.ShapeDtypeStruct((total, CELLS), jnp.float32),
        in_specs=[SMEM, HBM, HBM, HBM],
        out_specs=VMEM,
        scratch_shapes=[
            pltpu.VMEM((CX, orb.shape[0], CY), jnp.float32),
            pltpu.SMEM(occupied.shape, jnp.int32),
            pltpu.SemaphoreType.DMA((CX + 2,)),
        ],
        compiler_params=PARAMS,
        name="local_fields",
    )(block_index, occupied, psi, orb)


def join(phase, packs, planes):
    count = len(packs)
    field_rows = FIELDS * planes

    def body(phase_ref, *refs):
        ins, out = refs[:count], refs[count]
        cosine, sine = phase_rows(phase_ref)
        last = lax.broadcasted_iota(jnp.int32, (planes, CELLS), 0) == planes - 1

        def end(ref, e, c):
            return ref[pl.ds(field_rows + (2 * e + c) * BLOCK, BLOCK), :]

        for d in range(count):
            here, there = ins[d], ins[(d + 1) % count]
            out[pl.ds(d * field_rows, 4 * planes), :] = here[pl.ds(0, 4 * planes), :]
            re, im = bond(end(here, 1, 0), end(here, 1, 1), end(there, 0, 0), end(there, 0, 1))
            re = jnp.sum(re, axis=0, keepdims=True)
            im = jnp.sum(im, axis=0, keepdims=True)
            re = jnp.where(last, re, here[pl.ds(4 * planes, planes), :])
            im = jnp.where(last, im, here[pl.ds(5 * planes, planes), :])
            out[pl.ds(d * field_rows + 4 * planes, planes), :] = re * cosine + im * sine
            out[pl.ds(d * field_rows + 5 * planes, planes), :] = im * cosine - re * sine

    return pl.pallas_call(
        body,
        out_shape=jax.ShapeDtypeStruct((count * field_rows, CELLS), jnp.float32),
        in_specs=[VMEM] + [VMEM] * count,
        out_specs=VMEM,
        compiler_params=PARAMS,
        name="join_slabs",
    )(phase, *packs)


def apply(phase, parts, packs, planes, bands):
    count = len(packs)
    field_rows = FIELDS * planes
    psi_start = field_rows + 4 * BLOCK
    scale = 1.0 / (count * planes * CELLS)

    def body(phase_ref, *refs):
        part_refs, ins = refs[: len(parts)], refs[len(parts) : len(parts) + count]
        out_ref, tile_ref = refs[len(parts) + count :]
        cosine, sine = phase_rows(phase_ref)
        row = lax.broadcasted_iota(jnp.int32, (planes, CELLS), 0)

        def window(d, i, offset=0):
            at = pl.ds(d * field_rows + i * planes, planes)
            total = part_refs[0][at, :]
            for ref in part_refs[1:]:
                total = total + ref[at, :]
            return total

        def psi_at(d, b, c):
            return ins[d % count][pl.ds(psi_start + (2 * b + c) * planes, planes), :]

        def above(d, field):
            return jnp.where(row == planes - 1, pltpu.roll(field(d + 1), planes - 1, 0), pltpu.roll(field(d), planes - 1, 0))

        def below(d, field):
            return jnp.where(row == 0, pltpu.roll(field(d - 1), 1, 0), pltpu.roll(field(d), 1, 0))

        up = []
        for d in range(count):
            re, im = window(d, 4), window(d, 5)
            up.append((re * cosine - im * sine, im * cosine + re * sine))
        sums = [[[None, None] for _ in range(bands)] for _ in range(bands)]
        for d in range(count):
            dens = window(d, 0) * (1.0 / DIAG)
            dx_re, dx_im = halves(window(d, 1))
            x_re = jnp.concatenate([dx_re, dx_re], axis=1) * 2.0
            x_im = jnp.concatenate([dx_im, -dx_im], axis=1) * 2.0
            y_re, y_im = window(d, 2), window(d, 3)
            yb_re, yb_im = turn(y_re, -1), -turn(y_im, -1)
            z_re, z_im = up[d]
            zb_re = below(d, lambda e: up[e % count][0])
            zb_im = -below(d, lambda e: up[e % count][1])
            results = []
            for b in range(bands):
                re, im = psi_at(d, b, 0), psi_at(d, b, 1)
                acc_re = jnp.zeros_like(re)
                acc_im = jnp.zeros_like(re)
                terms = (
                    (x_re, x_im, swap_x(re), swap_x(im)),
                    (y_re, y_im, turn(re, 1), turn(im, 1)),
                    (yb_re, yb_im, turn(re, -1), turn(im, -1)),
                    (z_re, z_im, above(d, lambda e: psi_at(e, b, 0)), above(d, lambda e: psi_at(e, b, 1))),
                    (zb_re, zb_im, below(d, lambda e: psi_at(e, b, 0)), below(d, lambda e: psi_at(e, b, 1))),
                )
                for wr, wi, vr, vi in terms:
                    acc_re = acc_re + (wr * vr - wi * vi)
                    acc_im = acc_im + (wr * vi + wi * vr)
                out_re = -(dens * re + acc_re * (1.0 / (DIAG * DIAG)))
                out_im = -(dens * im + acc_im * (1.0 / (DIAG * DIAG)))
                results.append((out_re, out_im))
                if d == 0:
                    out_ref[pl.ds(2 * b * planes, planes), :] = out_re
                    out_ref[pl.ds((2 * b + 1) * planes, planes), :] = out_im
            for a in range(bands):
                re, im = psi_at(d, a, 0), psi_at(d, a, 1)
                for b in range(bands):
                    out_re, out_im = results[b]
                    both = (re * out_re + im * out_im, re * out_im - im * out_re)
                    for c in range(2):
                        old = sums[a][b][c]
                        sums[a][b][c] = both[c] if old is None else old + both[c]
        shape = (bands, 2)
        first = lax.broadcasted_iota(jnp.int32, shape, 0)
        second = lax.broadcasted_iota(jnp.int32, shape, 1)
        for a in range(bands):
            tile = jnp.zeros(shape, jnp.float32)
            for b in range(bands):
                for c in range(2):
                    folded = sums[a][b][c]
                    folded = folded[:, :CY] + folded[:, CY:]
                    value = jnp.sum(jnp.sum(folded, axis=0, keepdims=True), axis=1, keepdims=True)
                    tile = jnp.where((first == b) & (second == c), value * scale, tile)
            tile_ref[0, a] = tile

    return pl.pallas_call(
        body,
        out_shape=(
            jax.ShapeDtypeStruct((2 * bands * planes, CELLS), jnp.float32),
            jax.ShapeDtypeStruct((1, bands, bands, 2), jnp.float32),
        ),
        in_specs=[VMEM] + [VMEM] * (len(parts) + count),
        out_specs=(VMEM, VMEM),
        compiler_params=PARAMS,
        name="apply_window",
    )(phase, *parts, *packs)


def shift(value, axis, distance):
    count = lax.axis_size(axis)
    return lax.ppermute(value, axis, [((i + distance) % count, i) for i in range(count)])


def body(targets, orbitals, block_index, occupied, kpoint):
    bands, planes = targets.shape[1], targets.shape[3]
    cycle, slabs = lax.axis_size("kring"), lax.axis_size("slab")
    place = lax.axis_index("kring")
    psi = targets.reshape(2 * bands * planes, CELLS)
    orb = orbitals.reshape(-1, CELLS)

    phase = phase_of(kpoint, place, cycle)

    occupied, psi, orb = [pltpu.with_memory_space_constraint(v, pltpu.HBM) for v in (occupied, psi, orb)]
    own = gather(block_index, occupied, psi, orb, planes)
    packs = [own] + [shift(own, "slab", d) for d in range(1, slabs)]
    mine = join(phase, packs, planes)

    other = lax.ppermute(mine, "kring", [(i, i ^ 1) for i in range(cycle)])
    pair = mine + other
    even = lax.rem(place, 2) == 0
    right = shift(jnp.where(even, mine, pair), "kring", 2)
    left = shift(jnp.where(even, pair, mine), "kring", -2)
    exchange, tile = apply(phase, [pair, right, left], packs, planes, bands)
    return exchange.reshape(targets.shape), tile


def solution(mesh):
    placed = (
        P("kring", None, None, "slab", None),
        P("kring", None, None, "slab", None),
        P("kring"),
        P("kring", None),
        P(),
    )
    return jax.shard_map(
        body,
        mesh=mesh,
        in_specs=placed,
        out_specs=(P("kring", None, None, "slab", None), P("kring", None, None, None)),
        check_vma=False,
    )
```

```python
import math

import jax
import jax.numpy as jnp
from jax import lax
from jax.experimental import pallas as pl
from jax.experimental.pallas import tpu as pltpu
from jax.sharding import PartitionSpec as P

CX = 2
CY = 128
CELLS = CX * CY
BLOCK = 16
FIELDS = 6
CHUNKS = 2
DIAG = 7.0

VMEM = pl.BlockSpec(memory_space=pltpu.VMEM)
SMEM = pl.BlockSpec(memory_space=pltpu.SMEM)
HBM = pl.BlockSpec(memory_space=pltpu.HBM)
PARAMS = pltpu.CompilerParams(vmem_limit_bytes=4 * 1024 * 1024)


def halves(field):
    return field[:, :CY], field[:, CY:]


def turn(field, shift):
    a, b = halves(field)
    amount = (-shift) % CY
    return jnp.concatenate([pltpu.roll(a, amount, 1), pltpu.roll(b, amount, 1)], axis=1)


def swap_x(field):
    a, b = halves(field)
    return jnp.concatenate([b, a], axis=1)


def bond(ar, ai, br, bi):
    return ar * br + ai * bi, ai * br - ar * bi


def gather_kernel(planes, index_ref, occupied_hbm, psi_hbm, orb_hbm, pack_ref, psi_ref, orb, occupied_ref, sems):
    rows = 2 * planes
    field_rows = FIELDS * planes
    chunk = BLOCK // CHUNKS
    masks = pltpu.make_async_copy(occupied_hbm, occupied_ref, sems.at[0])
    masks.start()
    first = index_ref[0] * BLOCK
    loads = []
    for g in range(CHUNKS):
        source = pl.ds(pl.multiple_of((first + g * chunk) * rows, 8), chunk * rows)
        target = pl.ds(g * chunk * rows, chunk * rows)
        group = [
            pltpu.make_async_copy(
                orb_hbm.at[source, pl.ds(x * CY, CY)], orb.at[x, target], sems.at[2 + g * CX + x]
            )
            for x in range(CX)
        ]
        for load in group:
            load.start()
        loads.append(group)
    keep = pltpu.make_async_copy(psi_hbm, psi_ref, sems.at[1])
    keep.start()
    masks.wait()
    weights = [occupied_ref[0, first + m].astype(jnp.float32) for m in range(BLOCK)]
    band = lax.broadcasted_iota(jnp.int32, (BLOCK, 1), 0)
    column = jnp.zeros((BLOCK, 1), jnp.float32)
    for m in range(BLOCK):
        column = jnp.where(band == m, weights[m], column)
    none = jnp.zeros((planes, CY), jnp.float32)
    dens, dy_re, dy_im, dz_re, dz_im = [[none] * CX for _ in range(5)]
    dx_re, dx_im = none, none
    for m in range(BLOCK):
        if m % chunk == 0:
            for load in loads[m // chunk]:
                load.wait()
        re = [orb[x, pl.ds(m * rows, planes), :] * weights[m] for x in range(CX)]
        im = [orb[x, pl.ds(m * rows + planes, planes), :] * weights[m] for x in range(CX)]
        part = bond(re[0], im[0], re[1], im[1])
        dx_re, dx_im = dx_re + part[0], dx_im + part[1]
        for x in range(CX):
            dens[x] = dens[x] + (re[x] * re[x] + im[x] * im[x])
            part = bond(re[x], im[x], pltpu.roll(re[x], CY - 1, 1), pltpu.roll(im[x], CY - 1, 1))
            dy_re[x], dy_im[x] = dy_re[x] + part[0], dy_im[x] + part[1]
            part = bond(re[x], im[x], pltpu.roll(re[x], planes - 1, 0), pltpu.roll(im[x], planes - 1, 0))
            dz_re[x], dz_im[x] = dz_re[x] + part[0], dz_im[x] + part[1]
    for i, field in enumerate((dens, (dx_re, dx_im), dy_re, dy_im, dz_re, dz_im)):
        for x in range(CX):
            pack_ref[pl.ds(i * planes, planes), pl.ds(x * CY, CY)] = field[x]
    for e, plane in enumerate((0, planes - 1)):
        for c in range(2):
            for x in range(CX):
                ends = orb[x, pl.ds(c * planes + plane, BLOCK, stride=rows), :] * column
                pack_ref[pl.ds(field_rows + (2 * e + c) * BLOCK, BLOCK), pl.ds(x * CY, CY)] = ends
    keep.wait()


def gather(block_index, occupied, psi, orb, planes):
    def body(*refs):
        gather_kernel(planes, *refs)

    return pl.pallas_call(
        body,
        out_shape=(
            jax.ShapeDtypeStruct((FIELDS * planes + 4 * BLOCK, CELLS), jnp.float32),
            jax.ShapeDtypeStruct(psi.shape, jnp.float32),
        ),
        in_specs=[SMEM, HBM, HBM, HBM],
        out_specs=(VMEM, VMEM),
        scratch_shapes=[
            pltpu.VMEM((CX, 2 * planes * BLOCK, CY), jnp.float32),
            pltpu.SMEM(occupied.shape, jnp.int32),
            pltpu.SemaphoreType.DMA((2 + CX * CHUNKS,)),
        ],
        compiler_params=PARAMS,
        name="local_fields",
    )(block_index, occupied, psi, orb)


def phase_of(kpoint, place, cycle):
    def body(place_ref, kpoint_hbm, out_ref, labels, sem):
        load = pltpu.make_async_copy(kpoint_hbm, labels, sem)
        load.start()
        load.wait()
        label = labels[place_ref[0]].astype(jnp.float32)
        angle = jnp.full((8, CY), label * (2.0 * math.pi / cycle), jnp.float32)
        out_ref[pl.ds(0, 8), :] = jnp.cos(angle)
        out_ref[pl.ds(8, 8), :] = jnp.sin(angle)

    return pl.pallas_call(
        body,
        out_shape=jax.ShapeDtypeStruct((16, CY), jnp.float32),
        in_specs=[SMEM, HBM],
        out_specs=VMEM,
        scratch_shapes=[pltpu.SMEM(kpoint.shape, jnp.int32), pltpu.SemaphoreType.DMA],
        compiler_params=PARAMS,
        name="phase",
    )(place.reshape(1), kpoint)


def phase_rows(ref):
    return [jnp.concatenate([ref[pl.ds(8 * i, 1), :]] * CX, axis=1) for i in range(2)]


def stack(targets):
    rows = targets[0].shape[0]

    def body(*refs):
        for i, ref in enumerate(refs[:-1]):
            refs[-1][pl.ds(i * rows, rows), :] = ref[...]

    return pl.pallas_call(
        body,
        out_shape=jax.ShapeDtypeStruct((len(targets) * rows, CELLS), jnp.float32),
        in_specs=[VMEM] * len(targets),
        out_specs=VMEM,
        compiler_params=PARAMS,
        cost_estimate=pl.CostEstimate(flops=1000000000, bytes_accessed=0, transcendentals=0),
        name="stack_targets",
    )(*targets)


def join(phase, packs, planes):
    count = len(packs)
    field_rows = FIELDS * planes

    def body(phase_ref, *refs):
        ins, out = refs[:count], refs[count]
        cosine, sine = phase_rows(phase_ref)
        last = lax.broadcasted_iota(jnp.int32, (planes, CELLS), 0) == planes - 1

        def end(ref, e, c):
            return ref[pl.ds(field_rows + (2 * e + c) * BLOCK, BLOCK), :]

        for d in range(count):
            here, there = ins[d], ins[(d + 1) % count]
            out[pl.ds(d * field_rows, 4 * planes), :] = here[pl.ds(0, 4 * planes), :]
            re, im = bond(end(here, 1, 0), end(here, 1, 1), end(there, 0, 0), end(there, 0, 1))
            re = jnp.sum(re, axis=0, keepdims=True)
            im = jnp.sum(im, axis=0, keepdims=True)
            re = jnp.where(last, re, here[pl.ds(4 * planes, planes), :])
            im = jnp.where(last, im, here[pl.ds(5 * planes, planes), :])
            out[pl.ds(d * field_rows + 4 * planes, planes), :] = re * cosine + im * sine
            out[pl.ds(d * field_rows + 5 * planes, planes), :] = im * cosine - re * sine

    return pl.pallas_call(
        body,
        out_shape=jax.ShapeDtypeStruct((count * field_rows, CELLS), jnp.float32),
        in_specs=[VMEM] + [VMEM] * count,
        out_specs=VMEM,
        compiler_params=PARAMS,
        name="join_slabs",
    )(phase, *packs)


def apply(phase, parts, targets, planes, bands, count):
    field_rows = FIELDS * planes
    scale = 1.0 / (count * planes * CELLS)

    def body(phase_ref, *refs):
        part_refs, ins = refs[: len(parts)], refs[len(parts)]
        out_ref, tile_ref = refs[len(parts) + 1 :]
        cosine, sine = phase_rows(phase_ref)
        row = lax.broadcasted_iota(jnp.int32, (planes, CELLS), 0)

        def window(d, i, offset=0):
            at = pl.ds(d * field_rows + i * planes, planes)
            total = part_refs[0][at, :]
            for ref in part_refs[1:]:
                total = total + ref[at, :]
            return total

        def psi_at(d, b, c):
            return ins[pl.ds(((d % count) * 2 * bands + 2 * b + c) * planes, planes), :]

        def above(d, field):
            return jnp.where(row == planes - 1, pltpu.roll(field(d + 1), planes - 1, 0), pltpu.roll(field(d), planes - 1, 0))

        def below(d, field):
            return jnp.where(row == 0, pltpu.roll(field(d - 1), 1, 0), pltpu.roll(field(d), 1, 0))

        up = []
        for d in range(count):
            re, im = window(d, 4), window(d, 5)
            up.append((re * cosine - im * sine, im * cosine + re * sine))
        sums = [[[None, None] for _ in range(bands)] for _ in range(bands)]
        for d in range(count):
            dens = window(d, 0) * (1.0 / DIAG)
            dx_re, dx_im = halves(window(d, 1))
            x_re = jnp.concatenate([dx_re, dx_re], axis=1) * 2.0
            x_im = jnp.concatenate([dx_im, -dx_im], axis=1) * 2.0
            y_re, y_im = window(d, 2), window(d, 3)
            yb_re, yb_im = turn(y_re, -1), -turn(y_im, -1)
            z_re, z_im = up[d]
            zb_re = below(d, lambda e: up[e % count][0])
            zb_im = -below(d, lambda e: up[e % count][1])
            results = []
            for b in range(bands):
                re, im = psi_at(d, b, 0), psi_at(d, b, 1)
                acc_re = jnp.zeros_like(re)
                acc_im = jnp.zeros_like(re)
                terms = (
                    (x_re, x_im, swap_x(re), swap_x(im)),
                    (y_re, y_im, turn(re, 1), turn(im, 1)),
                    (yb_re, yb_im, turn(re, -1), turn(im, -1)),
                    (z_re, z_im, above(d, lambda e: psi_at(e, b, 0)), above(d, lambda e: psi_at(e, b, 1))),
                    (zb_re, zb_im, below(d, lambda e: psi_at(e, b, 0)), below(d, lambda e: psi_at(e, b, 1))),
                )
                for wr, wi, vr, vi in terms:
                    acc_re = acc_re + (wr * vr - wi * vi)
                    acc_im = acc_im + (wr * vi + wi * vr)
                out_re = -(dens * re + acc_re * (1.0 / (DIAG * DIAG)))
                out_im = -(dens * im + acc_im * (1.0 / (DIAG * DIAG)))
                results.append((out_re, out_im))
                if d == 0:
                    out_ref[pl.ds(2 * b * planes, planes), :] = out_re
                    out_ref[pl.ds((2 * b + 1) * planes, planes), :] = out_im
            for a in range(bands):
                re, im = psi_at(d, a, 0), psi_at(d, a, 1)
                for b in range(bands):
                    out_re, out_im = results[b]
                    both = (re * out_re + im * out_im, re * out_im - im * out_re)
                    for c in range(2):
                        old = sums[a][b][c]
                        sums[a][b][c] = both[c] if old is None else old + both[c]
        shape = (bands, 2)
        first = lax.broadcasted_iota(jnp.int32, shape, 0)
        second = lax.broadcasted_iota(jnp.int32, shape, 1)
        for a in range(bands):
            tile = jnp.zeros(shape, jnp.float32)
            for b in range(bands):
                for c in range(2):
                    folded = sums[a][b][c]
                    folded = folded[:, :CY] + folded[:, CY:]
                    value = jnp.sum(jnp.sum(folded, axis=0, keepdims=True), axis=1, keepdims=True)
                    tile = jnp.where((first == b) & (second == c), value * scale, tile)
            tile_ref[0, a] = tile

    return pl.pallas_call(
        body,
        out_shape=(
            jax.ShapeDtypeStruct((2 * bands * planes, CELLS), jnp.float32),
            jax.ShapeDtypeStruct((1, bands, bands, 2), jnp.float32),
        ),
        in_specs=[VMEM] * (len(parts) + 2),
        out_specs=(VMEM, VMEM),
        compiler_params=PARAMS,
        name="apply_window",
    )(phase, *parts, targets)


def shift(value, axis, distance):
    count = lax.axis_size(axis)
    return lax.ppermute(value, axis, [((i + distance) % count, i) for i in range(count)])


def body(targets, orbitals, block_index, occupied, kpoint):
    bands, planes = targets.shape[1], targets.shape[3]
    cycle, slabs = lax.axis_size("kring"), lax.axis_size("slab")
    place = lax.axis_index("kring")
    psi = targets.reshape(2 * bands * planes, CELLS)
    orb = orbitals.reshape(-1, CELLS)

    phase = phase_of(kpoint, place, cycle)

    occupied, psi, orb = [pltpu.with_memory_space_constraint(v, pltpu.HBM) for v in (occupied, psi, orb)]
    own, psi = gather(block_index, occupied, psi, orb, planes)
    packs = [own] + [shift(own, "slab", d) for d in range(1, slabs)]
    psis = [psi] + [shift(psi, "slab", d) for d in range(1, slabs)]
    mine = join(phase, packs, planes)

    left = shift(mine, "kring", -2)
    right = shift(mine, "kring", 2)
    even = lax.rem(place, 2) == 0
    lacking = mine + jnp.where(even, right, left)
    other = lax.ppermute(lacking, "kring", [(i, i ^ 1) for i in range(cycle)])
    other, psis = lax.optimization_barrier((other, stack(psis)))
    exchange, tile = apply(phase, [mine, left, right, other], psis, planes, bands, slabs)
    return exchange.reshape(targets.shape), tile


def solution(mesh):
    placed = (
        P("kring", None, None, "slab", None),
        P("kring", None, None, "slab", None),
        P("kring"),
        P("kring", None),
        P(),
    )
    return jax.shard_map(
        body,
        mesh=mesh,
        in_specs=placed,
        out_specs=(P("kring", None, None, "slab", None), P("kring", None, None, None)),
        check_vma=False,
    )
```

```python
import math

import jax
import jax.numpy as jnp
from jax import lax
from jax.experimental import pallas as pl
from jax.experimental.pallas import tpu as pltpu
from jax.sharding import PartitionSpec as P

CX = 2
CY = 128
CELLS = CX * CY
BLOCK = 16
FIELDS = 6
CHUNKS = 1
DIAG = 7.0

VMEM = pl.BlockSpec(memory_space=pltpu.VMEM)
SMEM = pl.BlockSpec(memory_space=pltpu.SMEM)
HBM = pl.BlockSpec(memory_space=pltpu.HBM)
PARAMS = pltpu.CompilerParams(vmem_limit_bytes=4 * 1024 * 1024)


def halves(field):
    return field[:, :CY], field[:, CY:]


def turn(field, shift):
    a, b = halves(field)
    amount = (-shift) % CY
    return jnp.concatenate([pltpu.roll(a, amount, 1), pltpu.roll(b, amount, 1)], axis=1)


def swap_x(field):
    a, b = halves(field)
    return jnp.concatenate([b, a], axis=1)


def bond(ar, ai, br, bi):
    return ar * br + ai * bi, ai * br - ar * bi


def gather_kernel(planes, index_ref, weight_ref, orb, pack_ref):
    rows = 2 * CX * planes
    field_rows = FIELDS * planes
    first = index_ref[0] * BLOCK
    none = jnp.zeros((planes, CY), jnp.float32)
    dens, dy_re, dy_im, dz_re, dz_im = [[none] * CX for _ in range(5)]
    dx_re, dx_im = none, none
    for m in range(BLOCK):
        base = pl.multiple_of((first + m) * rows, 8)
        weight = weight_ref[pl.ds(first + m, 1), :]
        re = [orb[pl.ds(base + x * planes, planes), :] * weight for x in range(CX)]
        im = [orb[pl.ds(base + (CX + x) * planes, planes), :] * weight for x in range(CX)]
        part = bond(re[0], im[0], re[1], im[1])
        dx_re, dx_im = dx_re + part[0], dx_im + part[1]
        for x in range(CX):
            dens[x] = dens[x] + (re[x] * re[x] + im[x] * im[x])
            part = bond(re[x], im[x], pltpu.roll(re[x], CY - 1, 1), pltpu.roll(im[x], CY - 1, 1))
            dy_re[x], dy_im[x] = dy_re[x] + part[0], dy_im[x] + part[1]
            part = bond(re[x], im[x], pltpu.roll(re[x], planes - 1, 0), pltpu.roll(im[x], planes - 1, 0))
            dz_re[x], dz_im[x] = dz_re[x] + part[0], dz_im[x] + part[1]
    for i, field in enumerate((dens, (dx_re, dx_im), dy_re, dy_im, dz_re, dz_im)):
        for x in range(CX):
            pack_ref[pl.ds(i * planes, planes), pl.ds(x * CY, CY)] = field[x]
    column = weight_ref[pl.ds(pl.multiple_of(first, BLOCK), BLOCK), :]
    for e, plane in enumerate((0, planes - 1)):
        for c in range(2):
            for x in range(CX):
                ends = orb[pl.ds(first * rows + (c * CX + x) * planes + plane, BLOCK, stride=rows), :] * column
                pack_ref[pl.ds(field_rows + (2 * e + c) * BLOCK, BLOCK), pl.ds(x * CY, CY)] = ends


def spread(occupied):
    count = occupied.shape[1]

    def body(occupied_hbm, out, masks, sem):
        load = pltpu.make_async_copy(occupied_hbm, masks, sem)
        load.start()
        band = lax.broadcasted_iota(jnp.int32, (count, count), 0)
        lane = lax.broadcasted_iota(jnp.int32, (count, count), 1)
        load.wait()
        chosen = jnp.where(band == lane, masks[...].astype(jnp.float32), 0.0)
        out[...] = jnp.broadcast_to(jnp.sum(chosen, axis=1, keepdims=True), (count, CY))

    return pl.pallas_call(
        body,
        out_shape=jax.ShapeDtypeStruct((count, CY), jnp.float32),
        in_specs=[HBM],
        out_specs=VMEM,
        scratch_shapes=[pltpu.VMEM(occupied.shape, jnp.int32), pltpu.SemaphoreType.DMA],
        compiler_params=PARAMS,
        cost_estimate=pl.CostEstimate(flops=1000000000, bytes_accessed=0, transcendentals=0),
        name="spread_mask",
    )(occupied)


def gather(block_index, weights, orb, planes):
    def body(*refs):
        gather_kernel(planes, *refs)

    return pl.pallas_call(
        body,
        out_shape=jax.ShapeDtypeStruct((FIELDS * planes + 4 * BLOCK, CELLS), jnp.float32),
        in_specs=[SMEM, VMEM, VMEM],
        out_specs=VMEM,
        compiler_params=PARAMS,
        name="local_fields",
    )(block_index, weights, orb)


def phase_of(kpoint, place, cycle):
    def body(place_ref, kpoint_hbm, out_ref, labels, sem):
        load = pltpu.make_async_copy(kpoint_hbm, labels, sem)
        load.start()
        load.wait()
        label = labels[place_ref[0]].astype(jnp.float32)
        angle = jnp.full((8, CY), label * (2.0 * math.pi / cycle), jnp.float32)
        out_ref[pl.ds(0, 8), :] = jnp.cos(angle)
        out_ref[pl.ds(8, 8), :] = jnp.sin(angle)

    return pl.pallas_call(
        body,
        out_shape=jax.ShapeDtypeStruct((16, CY), jnp.float32),
        in_specs=[SMEM, HBM],
        out_specs=VMEM,
        scratch_shapes=[pltpu.SMEM(kpoint.shape, jnp.int32), pltpu.SemaphoreType.DMA],
        compiler_params=PARAMS,
        name="phase",
    )(place.reshape(1), kpoint)


def phase_rows(ref):
    return [jnp.concatenate([ref[pl.ds(8 * i, 1), :]] * CX, axis=1) for i in range(2)]


def stack(targets):
    rows = targets[0].shape[0]

    def body(*refs):
        for i, ref in enumerate(refs[:-1]):
            refs[-1][pl.ds(i * rows, rows), :] = ref[...]

    return pl.pallas_call(
        body,
        out_shape=jax.ShapeDtypeStruct((len(targets) * rows, CELLS), jnp.float32),
        in_specs=[VMEM] * len(targets),
        out_specs=VMEM,
        compiler_params=PARAMS,
        cost_estimate=pl.CostEstimate(flops=1000000000, bytes_accessed=0, transcendentals=0),
        name="stack_targets",
    )(*targets)


def join(phase, packs, planes):
    count = len(packs)
    field_rows = FIELDS * planes

    def body(phase_ref, *refs):
        ins, out = refs[:count], refs[count]
        cosine, sine = phase_rows(phase_ref)
        last = lax.broadcasted_iota(jnp.int32, (planes, CELLS), 0) == planes - 1

        def end(ref, e, c):
            return ref[pl.ds(field_rows + (2 * e + c) * BLOCK, BLOCK), :]

        for d in range(count):
            here, there = ins[d], ins[(d + 1) % count]
            out[pl.ds(d * field_rows, 4 * planes), :] = here[pl.ds(0, 4 * planes), :]
            re, im = bond(end(here, 1, 0), end(here, 1, 1), end(there, 0, 0), end(there, 0, 1))
            re = jnp.sum(re, axis=0, keepdims=True)
            im = jnp.sum(im, axis=0, keepdims=True)
            re = jnp.where(last, re, here[pl.ds(4 * planes, planes), :])
            im = jnp.where(last, im, here[pl.ds(5 * planes, planes), :])
            out[pl.ds(d * field_rows + 4 * planes, planes), :] = re * cosine + im * sine
            out[pl.ds(d * field_rows + 5 * planes, planes), :] = im * cosine - re * sine

    return pl.pallas_call(
        body,
        out_shape=jax.ShapeDtypeStruct((count * field_rows, CELLS), jnp.float32),
        in_specs=[VMEM] + [VMEM] * count,
        out_specs=VMEM,
        compiler_params=PARAMS,
        name="join_slabs",
    )(phase, *packs)


def apply(phase, parts, targets, planes, bands, count):
    field_rows = FIELDS * planes
    scale = 1.0 / (count * planes * CELLS)

    def body(phase_ref, *refs):
        part_refs, ins = refs[: len(parts)], refs[len(parts)]
        out_ref, tile_ref = refs[len(parts) + 1 :]
        cosine, sine = phase_rows(phase_ref)
        row = lax.broadcasted_iota(jnp.int32, (planes, CELLS), 0)

        def window(d, i, offset=0):
            at = pl.ds(d * field_rows + i * planes, planes)
            total = part_refs[0][at, :]
            for ref in part_refs[1:]:
                total = total + ref[at, :]
            return total

        def psi_at(d, b, c):
            return ins[pl.ds(((d % count) * 2 * bands + 2 * b + c) * planes, planes), :]

        def above(d, field):
            return jnp.where(row == planes - 1, pltpu.roll(field(d + 1), planes - 1, 0), pltpu.roll(field(d), planes - 1, 0))

        def below(d, field):
            return jnp.where(row == 0, pltpu.roll(field(d - 1), 1, 0), pltpu.roll(field(d), 1, 0))

        up = []
        for d in range(count):
            re, im = window(d, 4), window(d, 5)
            up.append((re * cosine - im * sine, im * cosine + re * sine))
        sums = [[[None, None] for _ in range(bands)] for _ in range(bands)]
        for d in range(count):
            dens = window(d, 0) * (1.0 / DIAG)
            dx_re, dx_im = halves(window(d, 1))
            x_re = jnp.concatenate([dx_re, dx_re], axis=1) * 2.0
            x_im = jnp.concatenate([dx_im, -dx_im], axis=1) * 2.0
            y_re, y_im = window(d, 2), window(d, 3)
            yb_re, yb_im = turn(y_re, -1), -turn(y_im, -1)
            z_re, z_im = up[d]
            zb_re = below(d, lambda e: up[e % count][0])
            zb_im = -below(d, lambda e: up[e % count][1])
            results = []
            for b in range(bands):
                re, im = psi_at(d, b, 0), psi_at(d, b, 1)
                acc_re = jnp.zeros_like(re)
                acc_im = jnp.zeros_like(re)
                terms = (
                    (x_re, x_im, swap_x(re), swap_x(im)),
                    (y_re, y_im, turn(re, 1), turn(im, 1)),
                    (yb_re, yb_im, turn(re, -1), turn(im, -1)),
                    (z_re, z_im, above(d, lambda e: psi_at(e, b, 0)), above(d, lambda e: psi_at(e, b, 1))),
                    (zb_re, zb_im, below(d, lambda e: psi_at(e, b, 0)), below(d, lambda e: psi_at(e, b, 1))),
                )
                for wr, wi, vr, vi in terms:
                    acc_re = acc_re + (wr * vr - wi * vi)
                    acc_im = acc_im + (wr * vi + wi * vr)
                out_re = -(dens * re + acc_re * (1.0 / (DIAG * DIAG)))
                out_im = -(dens * im + acc_im * (1.0 / (DIAG * DIAG)))
                results.append((out_re, out_im))
                if d == 0:
                    out_ref[pl.ds(2 * b * planes, planes), :] = out_re
                    out_ref[pl.ds((2 * b + 1) * planes, planes), :] = out_im
            for a in range(bands):
                re, im = psi_at(d, a, 0), psi_at(d, a, 1)
                for b in range(bands):
                    out_re, out_im = results[b]
                    both = (re * out_re + im * out_im, re * out_im - im * out_re)
                    for c in range(2):
                        old = sums[a][b][c]
                        sums[a][b][c] = both[c] if old is None else old + both[c]
        shape = (bands, 2)
        first = lax.broadcasted_iota(jnp.int32, shape, 0)
        second = lax.broadcasted_iota(jnp.int32, shape, 1)
        for a in range(bands):
            tile = jnp.zeros(shape, jnp.float32)
            for b in range(bands):
                for c in range(2):
                    folded = sums[a][b][c]
                    folded = folded[:, :CY] + folded[:, CY:]
                    value = jnp.sum(jnp.sum(folded, axis=0, keepdims=True), axis=1, keepdims=True)
                    tile = jnp.where((first == b) & (second == c), value * scale, tile)
            tile_ref[0, a] = tile

    return pl.pallas_call(
        body,
        out_shape=(
            jax.ShapeDtypeStruct((2 * bands * planes, CELLS), jnp.float32),
            jax.ShapeDtypeStruct((1, bands, bands, 2), jnp.float32),
        ),
        in_specs=[VMEM] * (len(parts) + 2),
        out_specs=(VMEM, VMEM),
        compiler_params=PARAMS,
        name="apply_window",
    )(phase, *parts, targets)


def shift(value, axis, distance):
    count = lax.axis_size(axis)
    return lax.ppermute(value, axis, [((i + distance) % count, i) for i in range(count)])


def body(targets, orbitals, block_index, occupied, kpoint):
    bands, planes = targets.shape[1], targets.shape[3]
    cycle, slabs = lax.axis_size("kring"), lax.axis_size("slab")
    place = lax.axis_index("kring")
    psi = targets.reshape(2 * bands * planes, CELLS)
    orb = orbitals.reshape(-1, planes, CX, CY).transpose(0, 2, 1, 3).reshape(-1, CY)

    phase = phase_of(kpoint, place, cycle)

    occupied = pltpu.with_memory_space_constraint(occupied, pltpu.HBM)
    own = gather(block_index, spread(occupied), orb, planes)
    packs = [own] + [shift(own, "slab", d) for d in range(1, slabs)]
    psis = [psi] + [shift(psi, "slab", d) for d in range(1, slabs)]
    mine = join(phase, packs, planes)

    left = shift(mine, "kring", -2)
    right = shift(mine, "kring", 2)
    even = lax.rem(place, 2) == 0
    lacking = mine + jnp.where(even, right, left)
    other = lax.ppermute(lacking, "kring", [(i, i ^ 1) for i in range(cycle)])
    other, psis = lax.optimization_barrier((other, stack(psis)))
    exchange, tile = apply(phase, [mine, left, right, other], psis, planes, bands, slabs)
    return exchange.reshape(targets.shape), tile


def solution(mesh):
    placed = (
        P("kring", None, None, "slab", None),
        P("kring", None, None, "slab", None),
        P("kring"),
        P("kring", None),
        P(),
    )
    return jax.shard_map(
        body,
        mesh=mesh,
        in_specs=placed,
        out_specs=(P("kring", None, None, "slab", None), P("kring", None, None, None)),
        check_vma=False,
    )
```

```python
import math

import jax
import jax.numpy as jnp
from jax import lax
from jax.experimental import pallas as pl
from jax.experimental.pallas import tpu as pltpu
from jax.sharding import PartitionSpec as P

CX = 2
CY = 128
CELLS = CX * CY
BLOCK = 16
FIELDS = 6
CHUNKS = 1
DIAG = 7.0

VMEM = pl.BlockSpec(memory_space=pltpu.VMEM)
SMEM = pl.BlockSpec(memory_space=pltpu.SMEM)
HBM = pl.BlockSpec(memory_space=pltpu.HBM)
PARAMS = pltpu.CompilerParams(vmem_limit_bytes=4 * 1024 * 1024)


def halves(field):
    return field[:, :CY], field[:, CY:]


def turn(field, shift):
    a, b = halves(field)
    amount = (-shift) % CY
    return jnp.concatenate([pltpu.roll(a, amount, 1), pltpu.roll(b, amount, 1)], axis=1)


def swap_x(field):
    a, b = halves(field)
    return jnp.concatenate([b, a], axis=1)


def bond(ar, ai, br, bi):
    return ar * br + ai * bi, ai * br - ar * bi


def gather_kernel(planes, index_ref, weight_ref, orb, pack_ref):
    rows = 2 * CX * planes
    field_rows = FIELDS * planes
    first = index_ref[0] * BLOCK
    none = jnp.zeros((planes, CY), jnp.float32)
    dens, dy_re, dy_im, dz_re, dz_im = [[none] * CX for _ in range(5)]
    dx_re, dx_im = none, none
    for m in range(BLOCK):
        base = pl.multiple_of((first + m) * rows, 8)
        weight = weight_ref[pl.ds(first + m, 1), :]
        re = [orb[pl.ds(base + x * planes, planes), :] * weight for x in range(CX)]
        im = [orb[pl.ds(base + (CX + x) * planes, planes), :] * weight for x in range(CX)]
        part = bond(re[0], im[0], re[1], im[1])
        dx_re, dx_im = dx_re + part[0], dx_im + part[1]
        for x in range(CX):
            dens[x] = dens[x] + (re[x] * re[x] + im[x] * im[x])
            part = bond(re[x], im[x], pltpu.roll(re[x], CY - 1, 1), pltpu.roll(im[x], CY - 1, 1))
            dy_re[x], dy_im[x] = dy_re[x] + part[0], dy_im[x] + part[1]
            part = bond(re[x], im[x], pltpu.roll(re[x], planes - 1, 0), pltpu.roll(im[x], planes - 1, 0))
            dz_re[x], dz_im[x] = dz_re[x] + part[0], dz_im[x] + part[1]
    for i, field in enumerate((dens, (dx_re, dx_im), dy_re, dy_im, dz_re, dz_im)):
        for x in range(CX):
            pack_ref[pl.ds(i * planes, planes), pl.ds(x * CY, CY)] = field[x]
    column = weight_ref[pl.ds(pl.multiple_of(first, BLOCK), BLOCK), :]
    for e, plane in enumerate((0, planes - 1)):
        for c in range(2):
            for x in range(CX):
                ends = orb[pl.ds(first * rows + (c * CX + x) * planes + plane, BLOCK, stride=rows), :] * column
                pack_ref[pl.ds(field_rows + (2 * e + c) * BLOCK, BLOCK), pl.ds(x * CY, CY)] = ends


def diagonal(count):
    def body(out):
        row = lax.broadcasted_iota(jnp.int32, (count, count), 0)
        column = lax.broadcasted_iota(jnp.int32, (count, count), 1)
        out[...] = jnp.where(row == column, 1.0, 0.0)

    return pl.pallas_call(
        body,
        out_shape=jax.ShapeDtypeStruct((count, count), jnp.float32),
        out_specs=VMEM,
        compiler_params=PARAMS,
        cost_estimate=pl.CostEstimate(flops=1000000000, bytes_accessed=0, transcendentals=0),
        name="diagonal",
    )()


def spread(mask, ones):
    count = mask.shape[1]

    def body(mask_ref, ones_ref, out):
        held = jnp.sum(mask_ref[...] * ones_ref[...], axis=1, keepdims=True)
        out[...] = jnp.broadcast_to(held, (count, CY))

    return pl.pallas_call(
        body,
        out_shape=jax.ShapeDtypeStruct((count, CY), jnp.float32),
        in_specs=[VMEM, VMEM],
        out_specs=VMEM,
        compiler_params=PARAMS,
        name="spread_mask",
    )(mask, ones)


def gather(block_index, weights, orb, planes):
    def body(*refs):
        gather_kernel(planes, *refs)

    return pl.pallas_call(
        body,
        out_shape=jax.ShapeDtypeStruct((FIELDS * planes + 4 * BLOCK, CELLS), jnp.float32),
        in_specs=[SMEM, VMEM, VMEM],
        out_specs=VMEM,
        compiler_params=PARAMS,
        name="local_fields",
    )(block_index, weights, orb)


def phase_of(kpoint, place, cycle):
    def body(place_ref, kpoint_hbm, out_ref, labels, sem):
        load = pltpu.make_async_copy(kpoint_hbm, labels, sem)
        load.start()
        load.wait()
        label = labels[place_ref[0]].astype(jnp.float32)
        angle = jnp.full((8, CY), label * (2.0 * math.pi / cycle), jnp.float32)
        out_ref[pl.ds(0, 8), :] = jnp.cos(angle)
        out_ref[pl.ds(8, 8), :] = jnp.sin(angle)

    return pl.pallas_call(
        body,
        out_shape=jax.ShapeDtypeStruct((16, CY), jnp.float32),
        in_specs=[SMEM, HBM],
        out_specs=VMEM,
        scratch_shapes=[pltpu.SMEM(kpoint.shape, jnp.int32), pltpu.SemaphoreType.DMA],
        compiler_params=PARAMS,
        name="phase",
    )(place.reshape(1), kpoint)


def phase_rows(ref):
    return [jnp.concatenate([ref[pl.ds(8 * i, 1), :]] * CX, axis=1) for i in range(2)]


def stack(targets):
    rows = targets[0].shape[0]

    def body(*refs):
        for i, ref in enumerate(refs[:-1]):
            refs[-1][pl.ds(i * rows, rows), :] = ref[...]

    return pl.pallas_call(
        body,
        out_shape=jax.ShapeDtypeStruct((len(targets) * rows, CELLS), jnp.float32),
        in_specs=[VMEM] * len(targets),
        out_specs=VMEM,
        compiler_params=PARAMS,
        cost_estimate=pl.CostEstimate(flops=1000000000, bytes_accessed=0, transcendentals=0),
        name="stack_targets",
    )(*targets)


def join(phase, packs, planes):
    count = len(packs)
    field_rows = FIELDS * planes

    def body(phase_ref, *refs):
        ins, out = refs[:count], refs[count]
        cosine, sine = phase_rows(phase_ref)
        last = lax.broadcasted_iota(jnp.int32, (planes, CELLS), 0) == planes - 1

        def end(ref, e, c):
            return ref[pl.ds(field_rows + (2 * e + c) * BLOCK, BLOCK), :]

        for d in range(count):
            here, there = ins[d], ins[(d + 1) % count]
            out[pl.ds(d * field_rows, 4 * planes), :] = here[pl.ds(0, 4 * planes), :]
            re, im = bond(end(here, 1, 0), end(here, 1, 1), end(there, 0, 0), end(there, 0, 1))
            re = jnp.sum(re, axis=0, keepdims=True)
            im = jnp.sum(im, axis=0, keepdims=True)
            re = jnp.where(last, re, here[pl.ds(4 * planes, planes), :])
            im = jnp.where(last, im, here[pl.ds(5 * planes, planes), :])
            out[pl.ds(d * field_rows + 4 * planes, planes), :] = re * cosine + im * sine
            out[pl.ds(d * field_rows + 5 * planes, planes), :] = im * cosine - re * sine

    return pl.pallas_call(
        body,
        out_shape=jax.ShapeDtypeStruct((count * field_rows, CELLS), jnp.float32),
        in_specs=[VMEM] + [VMEM] * count,
        out_specs=VMEM,
        compiler_params=PARAMS,
        name="join_slabs",
    )(phase, *packs)


def apply(phase, parts, targets, planes, bands, count):
    field_rows = FIELDS * planes
    scale = 1.0 / (count * planes * CELLS)

    def body(phase_ref, *refs):
        part_refs, ins = refs[: len(parts)], refs[len(parts)]
        out_ref, tile_ref = refs[len(parts) + 1 :]
        cosine, sine = phase_rows(phase_ref)
        row = lax.broadcasted_iota(jnp.int32, (planes, CELLS), 0)

        def window(d, i, offset=0):
            at = pl.ds(d * field_rows + i * planes, planes)
            total = part_refs[0][at, :]
            for ref in part_refs[1:]:
                total = total + ref[at, :]
            return total

        def psi_at(d, b, c):
            return ins[pl.ds(((d % count) * 2 * bands + 2 * b + c) * planes, planes), :]

        def above(d, field):
            return jnp.where(row == planes - 1, pltpu.roll(field(d + 1), planes - 1, 0), pltpu.roll(field(d), planes - 1, 0))

        def below(d, field):
            return jnp.where(row == 0, pltpu.roll(field(d - 1), 1, 0), pltpu.roll(field(d), 1, 0))

        up = []
        for d in range(count):
            re, im = window(d, 4), window(d, 5)
            up.append((re * cosine - im * sine, im * cosine + re * sine))
        sums = [[[None, None] for _ in range(bands)] for _ in range(bands)]
        for d in range(count):
            dens = window(d, 0) * (1.0 / DIAG)
            dx_re, dx_im = halves(window(d, 1))
            x_re = jnp.concatenate([dx_re, dx_re], axis=1) * 2.0
            x_im = jnp.concatenate([dx_im, -dx_im], axis=1) * 2.0
            y_re, y_im = window(d, 2), window(d, 3)
            yb_re, yb_im = turn(y_re, -1), -turn(y_im, -1)
            z_re, z_im = up[d]
            zb_re = below(d, lambda e: up[e % count][0])
            zb_im = -below(d, lambda e: up[e % count][1])
            results = []
            for b in range(bands):
                re, im = psi_at(d, b, 0), psi_at(d, b, 1)
                acc_re = jnp.zeros_like(re)
                acc_im = jnp.zeros_like(re)
                terms = (
                    (x_re, x_im, swap_x(re), swap_x(im)),
                    (y_re, y_im, turn(re, 1), turn(im, 1)),
                    (yb_re, yb_im, turn(re, -1), turn(im, -1)),
                    (z_re, z_im, above(d, lambda e: psi_at(e, b, 0)), above(d, lambda e: psi_at(e, b, 1))),
                    (zb_re, zb_im, below(d, lambda e: psi_at(e, b, 0)), below(d, lambda e: psi_at(e, b, 1))),
                )
                for wr, wi, vr, vi in terms:
                    acc_re = acc_re + (wr * vr - wi * vi)
                    acc_im = acc_im + (wr * vi + wi * vr)
                out_re = -(dens * re + acc_re * (1.0 / (DIAG * DIAG)))
                out_im = -(dens * im + acc_im * (1.0 / (DIAG * DIAG)))
                results.append((out_re, out_im))
                if d == 0:
                    out_ref[pl.ds(2 * b * planes, planes), :] = out_re
                    out_ref[pl.ds((2 * b + 1) * planes, planes), :] = out_im
            for a in range(bands):
                re, im = psi_at(d, a, 0), psi_at(d, a, 1)
                for b in range(bands):
                    out_re, out_im = results[b]
                    both = (re * out_re + im * out_im, re * out_im - im * out_re)
                    for c in range(2):
                        old = sums[a][b][c]
                        sums[a][b][c] = both[c] if old is None else old + both[c]
        shape = (bands, 2)
        first = lax.broadcasted_iota(jnp.int32, shape, 0)
        second = lax.broadcasted_iota(jnp.int32, shape, 1)
        for a in range(bands):
            tile = jnp.zeros(shape, jnp.float32)
            for b in range(bands):
                for c in range(2):
                    folded = sums[a][b][c]
                    folded = folded[:, :CY] + folded[:, CY:]
                    value = jnp.sum(jnp.sum(folded, axis=0, keepdims=True), axis=1, keepdims=True)
                    tile = jnp.where((first == b) & (second == c), value * scale, tile)
            tile_ref[0, a] = tile

    return pl.pallas_call(
        body,
        out_shape=(
            jax.ShapeDtypeStruct((2 * bands * planes, CELLS), jnp.float32),
            jax.ShapeDtypeStruct((1, bands, bands, 2), jnp.float32),
        ),
        in_specs=[VMEM] * (len(parts) + 2),
        out_specs=(VMEM, VMEM),
        compiler_params=PARAMS,
        name="apply_window",
    )(phase, *parts, targets)


def shift(value, axis, distance):
    count = lax.axis_size(axis)
    return lax.ppermute(value, axis, [((i + distance) % count, i) for i in range(count)])


def body(targets, orbitals, block_index, occupied, kpoint):
    bands, planes = targets.shape[1], targets.shape[3]
    cycle, slabs = lax.axis_size("kring"), lax.axis_size("slab")
    place = lax.axis_index("kring")
    psi = targets.reshape(2 * bands * planes, CELLS)
    orb = orbitals.reshape(-1, planes, CX, CY).transpose(0, 2, 1, 3).reshape(-1, CY)

    phase = phase_of(kpoint, place, cycle)

    held = occupied.shape[1]
    words = occupied + 2 * lax.pad(block_index, jnp.int32(0), [(0, held - 1, 0)]).reshape(1, held)
    mask = (words & 1).astype(jnp.float32)
    own = gather(block_index, spread(mask, diagonal(held)), orb, planes)
    packs = [own] + [shift(own, "slab", d) for d in range(1, slabs)]
    psis = [psi] + [shift(psi, "slab", d) for d in range(1, slabs)]
    mine = join(phase, packs, planes)

    left = shift(mine, "kring", -2)
    right = shift(mine, "kring", 2)
    even = lax.rem(place, 2) == 0
    lacking = mine + jnp.where(even, right, left)
    other = lax.ppermute(lacking, "kring", [(i, i ^ 1) for i in range(cycle)])
    other, psis = lax.optimization_barrier((other, stack(psis)))
    exchange, tile = apply(phase, [mine, left, right, other], psis, planes, bands, slabs)
    return exchange.reshape(targets.shape), tile


def solution(mesh):
    placed = (
        P("kring", None, None, "slab", None),
        P("kring", None, None, "slab", None),
        P("kring"),
        P("kring", None),
        P(),
    )
    return jax.shard_map(
        body,
        mesh=mesh,
        in_specs=placed,
        out_specs=(P("kring", None, None, "slab", None), P("kring", None, None, None)),
        check_vma=False,
    )
```

```python
import math

import jax
import jax.numpy as jnp
from jax import lax
from jax.experimental import pallas as pl
from jax.experimental.pallas import tpu as pltpu
from jax.sharding import PartitionSpec as P

CX = 2
CY = 128
CELLS = CX * CY
BLOCK = 16
FIELDS = 6
NEIGHBOURS = 6
CHUNKS = 1
DIAG = 7.0

VMEM = pl.BlockSpec(memory_space=pltpu.VMEM)
SMEM = pl.BlockSpec(memory_space=pltpu.SMEM)
HBM = pl.BlockSpec(memory_space=pltpu.HBM)
PARAMS = pltpu.CompilerParams(vmem_limit_bytes=4 * 1024 * 1024)


def halves(field):
    return field[:, :CY], field[:, CY:]


def turn(field, shift):
    a, b = halves(field)
    amount = (-shift) % CY
    return jnp.concatenate([pltpu.roll(a, amount, 1), pltpu.roll(b, amount, 1)], axis=1)


def swap_x(field):
    a, b = halves(field)
    return jnp.concatenate([b, a], axis=1)


def bond(ar, ai, br, bi):
    return ar * br + ai * bi, ai * br - ar * bi


def gather_kernel(planes, index_ref, weight_ref, orb, pack_ref):
    rows = 2 * CX * planes
    field_rows = FIELDS * planes
    first = index_ref[0] * BLOCK
    none = jnp.zeros((planes, CY), jnp.float32)
    dens, dy_re, dy_im, dz_re, dz_im = [[none] * CX for _ in range(5)]
    dx_re, dx_im = none, none
    for m in range(BLOCK):
        base = pl.multiple_of((first + m) * rows, 8)
        weight = weight_ref[pl.ds(first + m, 1), :]
        re = [orb[pl.ds(base + x * planes, planes), :] * weight for x in range(CX)]
        im = [orb[pl.ds(base + (CX + x) * planes, planes), :] * weight for x in range(CX)]
        part = bond(re[0], im[0], re[1], im[1])
        dx_re, dx_im = dx_re + part[0], dx_im + part[1]
        for x in range(CX):
            dens[x] = dens[x] + (re[x] * re[x] + im[x] * im[x])
            part = bond(re[x], im[x], pltpu.roll(re[x], CY - 1, 1), pltpu.roll(im[x], CY - 1, 1))
            dy_re[x], dy_im[x] = dy_re[x] + part[0], dy_im[x] + part[1]
            part = bond(re[x], im[x], pltpu.roll(re[x], planes - 1, 0), pltpu.roll(im[x], planes - 1, 0))
            dz_re[x], dz_im[x] = dz_re[x] + part[0], dz_im[x] + part[1]
    for i, field in enumerate((dens, (dx_re, dx_im), dy_re, dy_im, dz_re, dz_im)):
        for x in range(CX):
            pack_ref[pl.ds(i * planes, planes), pl.ds(x * CY, CY)] = field[x]
    column = weight_ref[pl.ds(pl.multiple_of(first, BLOCK), BLOCK), :]
    for e, plane in enumerate((0, planes - 1)):
        for c in range(2):
            for x in range(CX):
                ends = orb[pl.ds(first * rows + (c * CX + x) * planes + plane, BLOCK, stride=rows), :] * column
                pack_ref[pl.ds(field_rows + (2 * e + c) * BLOCK, BLOCK), pl.ds(x * CY, CY)] = ends


def diagonal(count):
    def body(out):
        row = lax.broadcasted_iota(jnp.int32, (count, count), 0)
        column = lax.broadcasted_iota(jnp.int32, (count, count), 1)
        out[...] = jnp.where(row == column, 1.0, 0.0)

    return pl.pallas_call(
        body,
        out_shape=jax.ShapeDtypeStruct((count, count), jnp.float32),
        out_specs=VMEM,
        compiler_params=PARAMS,
        cost_estimate=pl.CostEstimate(flops=1000000000, bytes_accessed=0, transcendentals=0),
        name="diagonal",
    )()


def spread(mask, ones):
    count = mask.shape[1]

    def body(mask_ref, ones_ref, out):
        held = jnp.sum(mask_ref[...] * ones_ref[...], axis=1, keepdims=True)
        out[...] = jnp.broadcast_to(held, (count, CY))

    return pl.pallas_call(
        body,
        out_shape=jax.ShapeDtypeStruct((count, CY), jnp.float32),
        in_specs=[VMEM, VMEM],
        out_specs=VMEM,
        compiler_params=PARAMS,
        name="spread_mask",
    )(mask, ones)


def gather(block_index, weights, orb, planes):
    def body(*refs):
        gather_kernel(planes, *refs)

    return pl.pallas_call(
        body,
        out_shape=jax.ShapeDtypeStruct((FIELDS * planes + 4 * BLOCK, CELLS), jnp.float32),
        in_specs=[SMEM, VMEM, VMEM],
        out_specs=VMEM,
        compiler_params=PARAMS,
        name="local_fields",
    )(block_index, weights, orb)


def phase_of(kpoint, place, cycle):
    def body(place_ref, kpoint_hbm, out_ref, labels, sem):
        load = pltpu.make_async_copy(kpoint_hbm, labels, sem)
        load.start()
        load.wait()
        label = labels[place_ref[0]].astype(jnp.float32)
        angle = jnp.full((8, CY), label * (2.0 * math.pi / cycle), jnp.float32)
        out_ref[pl.ds(0, 8), :] = jnp.cos(angle)
        out_ref[pl.ds(8, 8), :] = jnp.sin(angle)

    return pl.pallas_call(
        body,
        out_shape=jax.ShapeDtypeStruct((16, CY), jnp.float32),
        in_specs=[SMEM, HBM],
        out_specs=VMEM,
        scratch_shapes=[pltpu.SMEM(kpoint.shape, jnp.int32), pltpu.SemaphoreType.DMA],
        compiler_params=PARAMS,
        name="phase",
    )(place.reshape(1), kpoint)


def phase_rows(ref):
    return [jnp.concatenate([ref[pl.ds(8 * i, 1), :]] * CX, axis=1) for i in range(2)]


def ready_targets(targets, planes, bands):
    count = len(targets)
    cells = count * planes * CELLS
    values = tile_values(bands)

    def body(*refs):
        ins, near_ref, weight_ref = refs[:count], refs[count], refs[count + 1]
        row = lax.broadcasted_iota(jnp.int32, (planes, CELLS), 0)

        def psi_at(d, b):
            return [ins[d % count][pl.ds((2 * b + c) * planes, planes), :] for c in range(2)]

        def above(d, b):
            here, next_slab = psi_at(d, b), psi_at(d + 1, b)
            return [
                jnp.where(row == planes - 1, pltpu.roll(n, planes - 1, 0), pltpu.roll(h, planes - 1, 0))
                for h, n in zip(here, next_slab)
            ]

        def below(d, b):
            here, last_slab = psi_at(d, b), psi_at(d - 1, b)
            return [jnp.where(row == 0, pltpu.roll(n, 1, 0), pltpu.roll(h, 1, 0)) for h, n in zip(here, last_slab)]

        for b in range(bands):
            here = psi_at(0, b)
            neighbours = (
                here,
                [swap_x(v) for v in here],
                [turn(v, 1) for v in here],
                [turn(v, -1) for v in here],
                above(0, b),
                below(0, b),
            )
            for n, pair in enumerate(neighbours):
                for c in range(2):
                    near_ref[pl.ds(((b * NEIGHBOURS + n) * 2 + c) * planes, planes), :] = pair[c]

        def put(d, q, i, value, scale):
            weight_ref[pl.ds(((d * len(values) + q) * FIELDS + i) * planes, planes), :] = value * scale

        def mixed(first, second, a, b, part):
            one = bond(*second[b], *first[a])
            if a == b:
                return 2.0 * one[0], -2.0 * one[1]
            two = bond(*second[a], *first[b])
            if part == 0:
                return one[0] + two[0], -(one[1] + two[1])
            return one[1] - two[1], one[0] - two[0]

        for d in range(count):
            here = [psi_at(d, b) for b in range(bands)]
            left = [[halves(v)[0] for v in pair] for pair in here]
            right = [[halves(v)[1] for v in pair] for pair in here]
            beside = [[turn(v, 1) for v in pair] for pair in here]
            over = [above(d, b) for b in range(bands)]
            for q, (a, b, part) in enumerate(values):
                put(d, q, 0, bond(*here[b], *here[a])[part], -1.0 / (DIAG * cells))
                scale = -1.0 / (DIAG * DIAG * cells)
                put(d, q, 1, jnp.concatenate(mixed(left, right, a, b, part), axis=1), 2.0 * scale)
                for i, other in ((2, beside), (4, over)):
                    for c, value in enumerate(mixed(here, other, a, b, part)):
                        put(d, q, i + c, value, scale)

    return pl.pallas_call(
        body,
        out_shape=(
            jax.ShapeDtypeStruct((bands * NEIGHBOURS * 2 * planes, CELLS), jnp.float32),
            jax.ShapeDtypeStruct((count * len(values) * FIELDS * planes, CELLS), jnp.float32),
        ),
        in_specs=[VMEM] * count,
        out_specs=(VMEM, VMEM),
        compiler_params=PARAMS,
        cost_estimate=pl.CostEstimate(flops=1000000000, bytes_accessed=0, transcendentals=0),
        name="ready_targets",
    )(*targets)


def tile_values(bands):
    return [(a, b, part) for a in range(bands) for b in range(a, bands) for part in range(2 if b > a else 1)]


def join(phase, packs, planes):
    count = len(packs)
    field_rows = FIELDS * planes

    def body(phase_ref, *refs):
        ins, out = refs[:count], refs[count]
        cosine, sine = phase_rows(phase_ref)
        last = lax.broadcasted_iota(jnp.int32, (planes, CELLS), 0) == planes - 1

        def end(ref, e, c):
            return ref[pl.ds(field_rows + (2 * e + c) * BLOCK, BLOCK), :]

        for d in range(count):
            here, there = ins[d], ins[(d + 1) % count]
            out[pl.ds(d * field_rows, 4 * planes), :] = here[pl.ds(0, 4 * planes), :]
            re, im = bond(end(here, 1, 0), end(here, 1, 1), end(there, 0, 0), end(there, 0, 1))
            re = jnp.sum(re, axis=0, keepdims=True)
            im = jnp.sum(im, axis=0, keepdims=True)
            re = jnp.where(last, re, here[pl.ds(4 * planes, planes), :])
            im = jnp.where(last, im, here[pl.ds(5 * planes, planes), :])
            out[pl.ds(d * field_rows + 4 * planes, planes), :] = re * cosine + im * sine
            out[pl.ds(d * field_rows + 5 * planes, planes), :] = im * cosine - re * sine

    return pl.pallas_call(
        body,
        out_shape=jax.ShapeDtypeStruct((count * field_rows, CELLS), jnp.float32),
        in_specs=[VMEM] + [VMEM] * count,
        out_specs=VMEM,
        compiler_params=PARAMS,
        name="join_slabs",
    )(phase, *packs)


def apply(phase, parts, near, weights, planes, bands, count):
    field_rows = FIELDS * planes
    values = tile_values(bands)

    def body(phase_ref, *refs):
        part_refs, near_ref, weight_ref = refs[: len(parts)], refs[len(parts)], refs[len(parts) + 1]
        out_ref, tile_ref = refs[len(parts) + 2 :]
        cosine, sine = phase_rows(phase_ref)
        row = lax.broadcasted_iota(jnp.int32, (planes, CELLS), 0)

        def window(d, i):
            at = pl.ds(d * field_rows + i * planes, planes)
            total = part_refs[0][at, :]
            for ref in part_refs[1:]:
                total = total + ref[at, :]
            return total

        fields = []
        for d in range(count):
            held = [window(d, i) for i in range(FIELDS)]
            re, im = held[4:]
            fields.append(held[:4] + [re * cosine - im * sine, im * cosine + re * sine])

        dens, x_both, y_re, y_im, z_re, z_im = fields[0]
        dx_re, dx_im = halves(x_both)
        below = [
            jnp.where(row == 0, pltpu.roll(fields[count - 1][i], 1, 0), pltpu.roll(fields[0][i], 1, 0)) for i in (4, 5)
        ]
        factors = (
            (jnp.concatenate([dx_re, dx_re], axis=1) * 2.0, jnp.concatenate([dx_im, -dx_im], axis=1) * 2.0),
            (y_re, y_im),
            (turn(y_re, -1), -turn(y_im, -1)),
            (z_re, z_im),
            (below[0], -below[1]),
        )
        dens = dens * DIAG
        for b in range(bands):
            around = [
                [near_ref[pl.ds(((b * NEIGHBOURS + n) * 2 + c) * planes, planes), :] for c in range(2)]
                for n in range(NEIGHBOURS)
            ]
            acc_re = dens * around[0][0]
            acc_im = dens * around[0][1]
            for (wr, wi), (vr, vi) in zip(factors, around[1:]):
                acc_re = acc_re + (wr * vr - wi * vi)
                acc_im = acc_im + (wr * vi + wi * vr)
            out_ref[pl.ds(2 * b * planes, planes), :] = acc_re * (-1.0 / (DIAG * DIAG))
            out_ref[pl.ds((2 * b + 1) * planes, planes), :] = acc_im * (-1.0 / (DIAG * DIAG))

        found = {}
        for q, key in enumerate(values):
            total = jnp.zeros((planes, CELLS), jnp.float32)
            for d in range(count):
                for i in range(FIELDS):
                    at = pl.ds(((d * len(values) + q) * FIELDS + i) * planes, planes)
                    total = total + fields[d][i] * weight_ref[at, :]
            total = jnp.sum(total[:, :CY] + total[:, CY:], axis=0, keepdims=True)
            found[key] = jnp.sum(total, axis=1, keepdims=True)
        shape = (bands, 2)
        first = lax.broadcasted_iota(jnp.int32, shape, 0)
        second = lax.broadcasted_iota(jnp.int32, shape, 1)
        for a in range(bands):
            tile = jnp.zeros(shape, jnp.float32)
            for b in range(bands):
                low, high = min(a, b), max(a, b)
                tile = jnp.where((first == b) & (second == 0), found[low, high, 0], tile)
                if a != b:
                    imaginary = found[low, high, 1]
                    tile = jnp.where((first == b) & (second == 1), imaginary if a < b else -imaginary, tile)
            tile_ref[0, a] = tile

    return pl.pallas_call(
        body,
        out_shape=(
            jax.ShapeDtypeStruct((2 * bands * planes, CELLS), jnp.float32),
            jax.ShapeDtypeStruct((1, bands, bands, 2), jnp.float32),
        ),
        in_specs=[VMEM] * (len(parts) + 3),
        out_specs=(VMEM, VMEM),
        compiler_params=PARAMS,
        name="apply_window",
    )(phase, *parts, near, weights)


def shift(value, axis, distance):
    count = lax.axis_size(axis)
    return lax.ppermute(value, axis, [((i + distance) % count, i) for i in range(count)])


def body(targets, orbitals, block_index, occupied, kpoint):
    bands, planes = targets.shape[1], targets.shape[3]
    cycle, slabs = lax.axis_size("kring"), lax.axis_size("slab")
    place = lax.axis_index("kring")
    psi = targets.reshape(2 * bands * planes, CELLS)
    orb = orbitals.reshape(-1, planes, CX, CY).transpose(0, 2, 1, 3).reshape(-1, CY)

    phase = phase_of(kpoint, place, cycle)

    held = occupied.shape[1]
    words = occupied + 2 * lax.pad(block_index, jnp.int32(0), [(0, held - 1, 0)]).reshape(1, held)
    mask = (words & 1).astype(jnp.float32)
    own = gather(block_index, spread(mask, diagonal(held)), orb, planes)
    packs = [own] + [shift(own, "slab", d) for d in range(1, slabs)]
    psis = [psi] + [shift(psi, "slab", d) for d in range(1, slabs)]
    mine = join(phase, packs, planes)

    left = shift(mine, "kring", -2)
    right = shift(mine, "kring", 2)
    even = lax.rem(place, 2) == 0
    lacking = mine + jnp.where(even, right, left)
    other = lax.ppermute(lacking, "kring", [(i, i ^ 1) for i in range(cycle)])
    other, near, weights = lax.optimization_barrier((other, *ready_targets(psis, planes, bands)))
    exchange, tile = apply(phase, [mine, right, left, other], near, weights, planes, bands, slabs)
    return exchange.reshape(targets.shape), tile


def solution(mesh):
    placed = (
        P("kring", None, None, "slab", None),
        P("kring", None, None, "slab", None),
        P("kring"),
        P("kring", None),
        P(),
    )
    return jax.shard_map(
        body,
        mesh=mesh,
        in_specs=placed,
        out_specs=(P("kring", None, None, "slab", None), P("kring", None, None, None)),
        check_vma=False,
    )
```

```python
import math

import jax
import jax.numpy as jnp
from jax import lax
from jax.experimental import pallas as pl
from jax.experimental.pallas import tpu as pltpu
from jax.sharding import PartitionSpec as P

CX = 2
CY = 128
CELLS = CX * CY
BLOCK = 16
FIELDS = 6
SENT = 5
NEIGHBOURS = 6
CHUNKS = 1
DIAG = 7.0

VMEM = pl.BlockSpec(memory_space=pltpu.VMEM)
SMEM = pl.BlockSpec(memory_space=pltpu.SMEM)
HBM = pl.BlockSpec(memory_space=pltpu.HBM)
PARAMS = pltpu.CompilerParams(vmem_limit_bytes=4 * 1024 * 1024)


def halves(field):
    return field[:, :CY], field[:, CY:]


def turn(field, shift):
    a, b = halves(field)
    amount = (-shift) % CY
    return jnp.concatenate([pltpu.roll(a, amount, 1), pltpu.roll(b, amount, 1)], axis=1)


def swap_x(field):
    a, b = halves(field)
    return jnp.concatenate([b, a], axis=1)


def bond(ar, ai, br, bi):
    return ar * br + ai * bi, ai * br - ar * bi


def gather_kernel(planes, index_ref, weight_ref, orb, own_ref, pack_ref):
    rows = 2 * CX * planes
    field_rows = SENT * planes
    first = index_ref[0] * BLOCK
    none = jnp.zeros((planes, CY), jnp.float32)
    dens, dy_re, dy_im, dz_re, dz_im = [[none] * CX for _ in range(5)]
    dx_re, dx_im = none, none
    for m in range(BLOCK):
        base = pl.multiple_of((first + m) * rows, 8)
        weight = weight_ref[pl.ds(first + m, 1), :]
        re = [orb[pl.ds(base + x * planes, planes), :] * weight for x in range(CX)]
        im = [orb[pl.ds(base + (CX + x) * planes, planes), :] * weight for x in range(CX)]
        part = bond(re[0], im[0], re[1], im[1])
        dx_re, dx_im = dx_re + part[0], dx_im + part[1]
        for x in range(CX):
            dens[x] = dens[x] + (re[x] * re[x] + im[x] * im[x])
            part = bond(re[x], im[x], pltpu.roll(re[x], CY - 1, 1), pltpu.roll(im[x], CY - 1, 1))
            dy_re[x], dy_im[x] = dy_re[x] + part[0], dy_im[x] + part[1]
            part = bond(re[x], im[x], pltpu.roll(re[x], planes - 1, 0), pltpu.roll(im[x], planes - 1, 0))
            dz_re[x], dz_im[x] = dz_re[x] + part[0], dz_im[x] + part[1]
    row = lax.broadcasted_iota(jnp.int32, (planes, CY), 0)
    for i, field in enumerate((dens, (dx_re, dx_im), dy_re, dy_im, dz_re, dz_im)):
        for x in range(CX):
            own_ref[pl.ds(i * planes, planes), pl.ds(x * CY, CY)] = field[x]
            if i == SENT:
                continue
            sent = field[x]
            if i < SENT - 1:
                low = pltpu.roll(dz_im[x], (-2 * i) % planes, 0)
                high = pltpu.roll(dz_im[x], (planes - 2 - 2 * i) % planes, 0)
                sent = jnp.where(row == 0, low, jnp.where(row == planes - 1, high, sent))
            pack_ref[pl.ds(i * planes, planes), pl.ds(x * CY, CY)] = sent
    column = weight_ref[pl.ds(pl.multiple_of(first, BLOCK), BLOCK), :]
    for e, plane in enumerate((0, planes - 1)):
        for c in range(2):
            for x in range(CX):
                ends = orb[pl.ds(first * rows + (c * CX + x) * planes + plane, BLOCK, stride=rows), :] * column
                pack_ref[pl.ds(field_rows + (2 * e + c) * BLOCK, BLOCK), pl.ds(x * CY, CY)] = ends


def diagonal(count):
    def body(out):
        row = lax.broadcasted_iota(jnp.int32, (count, count), 0)
        column = lax.broadcasted_iota(jnp.int32, (count, count), 1)
        out[...] = jnp.where(row == column, 1.0, 0.0)

    return pl.pallas_call(
        body,
        out_shape=jax.ShapeDtypeStruct((count, count), jnp.float32),
        out_specs=VMEM,
        compiler_params=PARAMS,
        cost_estimate=pl.CostEstimate(flops=1000000000, bytes_accessed=0, transcendentals=0),
        name="diagonal",
    )()


def spread(mask, ones):
    count = mask.shape[1]

    def body(mask_ref, ones_ref, out):
        held = jnp.sum(mask_ref[...] * ones_ref[...], axis=1, keepdims=True)
        out[...] = jnp.broadcast_to(held, (count, CY))

    return pl.pallas_call(
        body,
        out_shape=jax.ShapeDtypeStruct((count, CY), jnp.float32),
        in_specs=[VMEM, VMEM],
        out_specs=VMEM,
        compiler_params=PARAMS,
        name="spread_mask",
    )(mask, ones)


def gather(block_index, weights, orb, planes):
    def body(*refs):
        gather_kernel(planes, *refs)

    return pl.pallas_call(
        body,
        out_shape=(
            jax.ShapeDtypeStruct((FIELDS * planes, CELLS), jnp.float32),
            jax.ShapeDtypeStruct((SENT * planes + 4 * BLOCK, CELLS), jnp.float32),
        ),
        in_specs=[SMEM, VMEM, VMEM],
        out_specs=(VMEM, VMEM),
        compiler_params=PARAMS,
        name="local_fields",
    )(block_index, weights, orb)


def phase_of(kpoint, place, cycle):
    def body(place_ref, kpoint_hbm, out_ref, labels, sem):
        load = pltpu.make_async_copy(kpoint_hbm, labels, sem)
        load.start()
        load.wait()
        label = labels[place_ref[0]].astype(jnp.float32)
        angle = jnp.full((8, CY), label * (2.0 * math.pi / cycle), jnp.float32)
        out_ref[pl.ds(0, 8), :] = jnp.cos(angle)
        out_ref[pl.ds(8, 8), :] = jnp.sin(angle)

    return pl.pallas_call(
        body,
        out_shape=jax.ShapeDtypeStruct((16, CY), jnp.float32),
        in_specs=[SMEM, HBM],
        out_specs=VMEM,
        scratch_shapes=[pltpu.SMEM(kpoint.shape, jnp.int32), pltpu.SemaphoreType.DMA],
        compiler_params=PARAMS,
        name="phase",
    )(place.reshape(1), kpoint)


def phase_rows(ref):
    return [jnp.concatenate([ref[pl.ds(8 * i, 1), :]] * CX, axis=1) for i in range(2)]


def ready_targets(targets, planes, bands):
    count = len(targets)
    cells = count * planes * CELLS
    values = tile_values(bands)

    def body(*refs):
        ins, near_ref, weight_ref = refs[:count], refs[count], refs[count + 1]
        row = lax.broadcasted_iota(jnp.int32, (planes, CELLS), 0)

        def psi_at(d, b):
            return [ins[d % count][pl.ds((2 * b + c) * planes, planes), :] for c in range(2)]

        def above(d, b):
            here, next_slab = psi_at(d, b), psi_at(d + 1, b)
            return [
                jnp.where(row == planes - 1, pltpu.roll(n, planes - 1, 0), pltpu.roll(h, planes - 1, 0))
                for h, n in zip(here, next_slab)
            ]

        def below(d, b):
            here, last_slab = psi_at(d, b), psi_at(d - 1, b)
            return [jnp.where(row == 0, pltpu.roll(n, 1, 0), pltpu.roll(h, 1, 0)) for h, n in zip(here, last_slab)]

        for b in range(bands):
            here = psi_at(0, b)
            neighbours = (
                here,
                [swap_x(v) for v in here],
                [turn(v, 1) for v in here],
                [turn(v, -1) for v in here],
                above(0, b),
                below(0, b),
            )
            for n, pair in enumerate(neighbours):
                for c in range(2):
                    near_ref[pl.ds(((b * NEIGHBOURS + n) * 2 + c) * planes, planes), :] = pair[c]

        def put(d, q, i, value, scale):
            weight_ref[pl.ds(((d * len(values) + q) * FIELDS + i) * planes, planes), :] = value * scale

        def mixed(first, second, a, b, part):
            one = bond(*second[b], *first[a])
            if a == b:
                return 2.0 * one[0], -2.0 * one[1]
            two = bond(*second[a], *first[b])
            if part == 0:
                return one[0] + two[0], -(one[1] + two[1])
            return one[1] - two[1], one[0] - two[0]

        for d in range(count):
            here = [psi_at(d, b) for b in range(bands)]
            left = [[halves(v)[0] for v in pair] for pair in here]
            right = [[halves(v)[1] for v in pair] for pair in here]
            beside = [[turn(v, 1) for v in pair] for pair in here]
            over = [above(d, b) for b in range(bands)]
            for q, (a, b, part) in enumerate(values):
                put(d, q, 0, bond(*here[b], *here[a])[part], -1.0 / (DIAG * cells))
                scale = -1.0 / (DIAG * DIAG * cells)
                put(d, q, 1, jnp.concatenate(mixed(left, right, a, b, part), axis=1), 2.0 * scale)
                for i, other in ((2, beside), (4, over)):
                    for c, value in enumerate(mixed(here, other, a, b, part)):
                        put(d, q, i + c, value, scale)

    return pl.pallas_call(
        body,
        out_shape=(
            jax.ShapeDtypeStruct((bands * NEIGHBOURS * 2 * planes, CELLS), jnp.float32),
            jax.ShapeDtypeStruct((count * len(values) * FIELDS * planes, CELLS), jnp.float32),
        ),
        in_specs=[VMEM] * count,
        out_specs=(VMEM, VMEM),
        compiler_params=PARAMS,
        cost_estimate=pl.CostEstimate(flops=1000000000, bytes_accessed=0, transcendentals=0),
        name="ready_targets",
    )(*targets)


def tile_values(bands):
    return [(a, b, part) for a in range(bands) for b in range(a, bands) for part in range(2 if b > a else 1)]


def join(phase, own, packs, planes):
    count = len(packs)
    field_rows = FIELDS * planes

    def body(phase_ref, own_ref, *refs):
        ins, out = refs[:count], refs[count]
        cosine, sine = phase_rows(phase_ref)
        row = lax.broadcasted_iota(jnp.int32, (planes, CELLS), 0)

        def total(value):
            return jnp.sum(value, axis=0, keepdims=True)

        def end(ref, e):
            return [ref[pl.ds(SENT * planes + (2 * e + c) * BLOCK, BLOCK), :] for c in range(2)]

        def rebuilt(ref):
            held = [ref[pl.ds(i * planes, planes), :] for i in range(SENT)]
            last = held[0]
            for i in range(SENT - 1):
                last = jnp.where(row == 2 * i, pltpu.roll(held[i], 2 * i, 0), last)
                last = jnp.where(row == 2 * i + 1, pltpu.roll(held[i], (2 * i + 2 - planes) % planes, 0), last)
            for e, place in ((0, 0), (1, planes - 1)):
                re, im = end(ref, e)
                (re0, re1), (im0, im1) = halves(re), halves(im)
                values = (
                    re * re + im * im,
                    jnp.concatenate(bond(re0, im0, re1, im1), axis=1),
                    *bond(re, im, turn(re, 1), turn(im, 1)),
                )
                for i, value in enumerate(values):
                    held[i] = jnp.where(row == place, total(value), held[i])
            return held + [last]

        for d in range(count):
            here, there = ins[d], ins[(d + 1) % count]
            if d == 0:
                held = [own_ref[pl.ds(i * planes, planes), :] for i in range(FIELDS)]
            else:
                held = rebuilt(here)
            re, im = bond(*end(here, 1), *end(there, 0))
            re = jnp.where(row == planes - 1, total(re), held[4])
            im = jnp.where(row == planes - 1, total(im), held[5])
            held[4:] = [re * cosine + im * sine, im * cosine - re * sine]
            for i, field in enumerate(held):
                out[pl.ds(d * field_rows + i * planes, planes), :] = field

    return pl.pallas_call(
        body,
        out_shape=jax.ShapeDtypeStruct((count * field_rows, CELLS), jnp.float32),
        in_specs=[VMEM] * (2 + count),
        out_specs=VMEM,
        compiler_params=PARAMS,
        name="join_slabs",
    )(phase, own, *packs)


def apply(phase, parts, near, weights, planes, bands, count):
    field_rows = FIELDS * planes
    values = tile_values(bands)

    def body(phase_ref, *refs):
        part_refs, near_ref, weight_ref = refs[: len(parts)], refs[len(parts)], refs[len(parts) + 1]
        out_ref, tile_ref = refs[len(parts) + 2 :]
        cosine, sine = phase_rows(phase_ref)
        row = lax.broadcasted_iota(jnp.int32, (planes, CELLS), 0)

        def window(d, i):
            at = pl.ds(d * field_rows + i * planes, planes)
            total = part_refs[0][at, :]
            for ref in part_refs[1:]:
                total = total + ref[at, :]
            return total

        fields = []
        for d in range(count):
            held = [window(d, i) for i in range(FIELDS)]
            re, im = held[4:]
            fields.append(held[:4] + [re * cosine - im * sine, im * cosine + re * sine])

        dens, x_both, y_re, y_im, z_re, z_im = fields[0]
        dx_re, dx_im = halves(x_both)
        below = [
            jnp.where(row == 0, pltpu.roll(fields[count - 1][i], 1, 0), pltpu.roll(fields[0][i], 1, 0)) for i in (4, 5)
        ]
        factors = (
            (jnp.concatenate([dx_re, dx_re], axis=1) * 2.0, jnp.concatenate([dx_im, -dx_im], axis=1) * 2.0),
            (y_re, y_im),
            (turn(y_re, -1), -turn(y_im, -1)),
            (z_re, z_im),
            (below[0], -below[1]),
        )
        dens = dens * DIAG
        for b in range(bands):
            around = [
                [near_ref[pl.ds(((b * NEIGHBOURS + n) * 2 + c) * planes, planes), :] for c in range(2)]
                for n in range(NEIGHBOURS)
            ]
            acc_re = dens * around[0][0]
            acc_im = dens * around[0][1]
            for (wr, wi), (vr, vi) in zip(factors, around[1:]):
                acc_re = acc_re + (wr * vr - wi * vi)
                acc_im = acc_im + (wr * vi + wi * vr)
            out_ref[pl.ds(2 * b * planes, planes), :] = acc_re * (-1.0 / (DIAG * DIAG))
            out_ref[pl.ds((2 * b + 1) * planes, planes), :] = acc_im * (-1.0 / (DIAG * DIAG))

        found = {}
        for q, key in enumerate(values):
            total = jnp.zeros((planes, CELLS), jnp.float32)
            for d in range(count):
                for i in range(FIELDS):
                    at = pl.ds(((d * len(values) + q) * FIELDS + i) * planes, planes)
                    total = total + fields[d][i] * weight_ref[at, :]
            total = jnp.sum(total[:, :CY] + total[:, CY:], axis=0, keepdims=True)
            found[key] = jnp.sum(total, axis=1, keepdims=True)
        shape = (bands, 2)
        first = lax.broadcasted_iota(jnp.int32, shape, 0)
        second = lax.broadcasted_iota(jnp.int32, shape, 1)
        for a in range(bands):
            tile = jnp.zeros(shape, jnp.float32)
            for b in range(bands):
                low, high = min(a, b), max(a, b)
                tile = jnp.where((first == b) & (second == 0), found[low, high, 0], tile)
                if a != b:
                    imaginary = found[low, high, 1]
                    tile = jnp.where((first == b) & (second == 1), imaginary if a < b else -imaginary, tile)
            tile_ref[0, a] = tile

    return pl.pallas_call(
        body,
        out_shape=(
            jax.ShapeDtypeStruct((2 * bands * planes, CELLS), jnp.float32),
            jax.ShapeDtypeStruct((1, bands, bands, 2), jnp.float32),
        ),
        in_specs=[VMEM] * (len(parts) + 3),
        out_specs=(VMEM, VMEM),
        compiler_params=PARAMS,
        name="apply_window",
    )(phase, *parts, near, weights)


def shift(value, axis, distance):
    count = lax.axis_size(axis)
    return lax.ppermute(value, axis, [((i + distance) % count, i) for i in range(count)])


def body(targets, orbitals, block_index, occupied, kpoint):
    bands, planes = targets.shape[1], targets.shape[3]
    cycle, slabs = lax.axis_size("kring"), lax.axis_size("slab")
    place = lax.axis_index("kring")
    psi = targets.reshape(2 * bands * planes, CELLS)
    orb = orbitals.reshape(-1, planes, CX, CY).transpose(0, 2, 1, 3).reshape(-1, CY)

    phase = phase_of(kpoint, place, cycle)

    held = occupied.shape[1]
    words = occupied + 2 * lax.pad(block_index, jnp.int32(0), [(0, held - 1, 0)]).reshape(1, held)
    mask = (words & 1).astype(jnp.float32)
    own, pack = gather(block_index, spread(mask, diagonal(held)), orb, planes)
    packs = [pack] + [shift(pack, "slab", d) for d in range(1, slabs)]
    psis = [psi] + [shift(psi, "slab", d) for d in range(1, slabs)]
    mine = join(phase, own, packs, planes)

    left = shift(mine, "kring", -2)
    right = shift(mine, "kring", 2)
    even = lax.rem(place, 2) == 0
    lacking = mine + jnp.where(even, right, left)
    other = lax.ppermute(lacking, "kring", [(i, i ^ 1) for i in range(cycle)])
    other, near, weights = lax.optimization_barrier((other, *ready_targets(psis, planes, bands)))
    exchange, tile = apply(phase, [mine, right, left, other], near, weights, planes, bands, slabs)
    return exchange.reshape(targets.shape), tile


def solution(mesh):
    placed = (
        P("kring", None, None, "slab", None),
        P("kring", None, None, "slab", None),
        P("kring"),
        P("kring", None),
        P(),
    )
    return jax.shard_map(
        body,
        mesh=mesh,
        in_specs=placed,
        out_specs=(P("kring", None, None, "slab", None), P("kring", None, None, None)),
        check_vma=False,
    )
```

```python
import math

import jax
import jax.numpy as jnp
from jax import lax
from jax.experimental import pallas as pl
from jax.experimental.pallas import tpu as pltpu
from jax.sharding import PartitionSpec as P

CX = 2
CY = 128
CELLS = CX * CY
BLOCK = 16
FIELDS = 6
SENT = 5
NEIGHBOURS = 6
CHUNKS = 1
DIAG = 7.0

VMEM = pl.BlockSpec(memory_space=pltpu.VMEM)
SMEM = pl.BlockSpec(memory_space=pltpu.SMEM)
HBM = pl.BlockSpec(memory_space=pltpu.HBM)
PARAMS = pltpu.CompilerParams(vmem_limit_bytes=4 * 1024 * 1024)


def halves(field):
    return field[:, :CY], field[:, CY:]


def turn(field, shift):
    a, b = halves(field)
    amount = (-shift) % CY
    return jnp.concatenate([pltpu.roll(a, amount, 1), pltpu.roll(b, amount, 1)], axis=1)


def swap_x(field):
    a, b = halves(field)
    return jnp.concatenate([b, a], axis=1)


def bond(ar, ai, br, bi):
    return ar * br + ai * bi, ai * br - ar * bi


def gather_kernel(planes, index_ref, weight_ref, orb, own_ref, pack_ref):
    rows = 2 * CX * planes
    field_rows = SENT * planes
    first = index_ref[0] * BLOCK
    none = jnp.zeros((planes, CY), jnp.float32)
    dens, dy_re, dy_im, dz_re, dz_im = [[none] * CX for _ in range(5)]
    dx_re, dx_im = none, none
    for m in range(BLOCK):
        base = pl.multiple_of((first + m) * rows, 8)
        weight = weight_ref[pl.ds(first + m, 1), :]
        raw_re = [orb[pl.ds(base + x * planes, planes), :] for x in range(CX)]
        raw_im = [orb[pl.ds(base + (CX + x) * planes, planes), :] for x in range(CX)]
        re = [value * weight for value in raw_re]
        im = [value * weight for value in raw_im]
        part = bond(re[0], im[0], raw_re[1], raw_im[1])
        dx_re, dx_im = dx_re + part[0], dx_im + part[1]
        for x in range(CX):
            dens[x] = dens[x] + (re[x] * raw_re[x] + im[x] * raw_im[x])
            part = bond(re[x], im[x], pltpu.roll(raw_re[x], CY - 1, 1), pltpu.roll(raw_im[x], CY - 1, 1))
            dy_re[x], dy_im[x] = dy_re[x] + part[0], dy_im[x] + part[1]
            part = bond(re[x], im[x], pltpu.roll(raw_re[x], planes - 1, 0), pltpu.roll(raw_im[x], planes - 1, 0))
            dz_re[x], dz_im[x] = dz_re[x] + part[0], dz_im[x] + part[1]
    row = lax.broadcasted_iota(jnp.int32, (planes, CY), 0)
    for i, field in enumerate((dens, (dx_re, dx_im), dy_re, dy_im, dz_re, dz_im)):
        for x in range(CX):
            own_ref[pl.ds(i * planes, planes), pl.ds(x * CY, CY)] = field[x]
            if i == SENT:
                continue
            sent = field[x]
            if i < SENT - 1:
                low = pltpu.roll(dz_im[x], (-2 * i) % planes, 0)
                high = pltpu.roll(dz_im[x], (planes - 2 - 2 * i) % planes, 0)
                sent = jnp.where(row == 0, low, jnp.where(row == planes - 1, high, sent))
            pack_ref[pl.ds(i * planes, planes), pl.ds(x * CY, CY)] = sent
    column = weight_ref[pl.ds(pl.multiple_of(first, BLOCK), BLOCK), :]
    for e, plane in enumerate((0, planes - 1)):
        for c in range(2):
            for x in range(CX):
                ends = orb[pl.ds(first * rows + (c * CX + x) * planes + plane, BLOCK, stride=rows), :] * column
                pack_ref[pl.ds(field_rows + (2 * e + c) * BLOCK, BLOCK), pl.ds(x * CY, CY)] = ends


def diagonal(count):
    def body(out):
        row = lax.broadcasted_iota(jnp.int32, (count, count), 0)
        column = lax.broadcasted_iota(jnp.int32, (count, count), 1)
        out[...] = jnp.where(row == column, 1.0, 0.0)

    return pl.pallas_call(
        body,
        out_shape=jax.ShapeDtypeStruct((count, count), jnp.float32),
        out_specs=VMEM,
        compiler_params=PARAMS,
        cost_estimate=pl.CostEstimate(flops=1000000000, bytes_accessed=0, transcendentals=0),
        name="diagonal",
    )()


def spread(mask, ones):
    count = mask.shape[1]

    def body(mask_ref, ones_ref, out):
        held = jnp.sum(mask_ref[...] * ones_ref[...], axis=1, keepdims=True)
        out[...] = jnp.broadcast_to(held, (count, CY))

    return pl.pallas_call(
        body,
        out_shape=jax.ShapeDtypeStruct((count, CY), jnp.float32),
        in_specs=[VMEM, VMEM],
        out_specs=VMEM,
        compiler_params=PARAMS,
        name="spread_mask",
    )(mask, ones)


def gather(block_index, weights, orb, planes):
    def body(*refs):
        gather_kernel(planes, *refs)

    return pl.pallas_call(
        body,
        out_shape=(
            jax.ShapeDtypeStruct((FIELDS * planes, CELLS), jnp.float32),
            jax.ShapeDtypeStruct((SENT * planes + 4 * BLOCK, CELLS), jnp.float32),
        ),
        in_specs=[SMEM, VMEM, VMEM],
        out_specs=(VMEM, VMEM),
        compiler_params=PARAMS,
        name="local_fields",
    )(block_index, weights, orb)


def phase_of(kpoint, place, cycle):
    def body(place_ref, kpoint_hbm, out_ref, labels, sem):
        load = pltpu.make_async_copy(kpoint_hbm, labels, sem)
        load.start()
        load.wait()
        label = labels[place_ref[0]].astype(jnp.float32)
        angle = jnp.full((8, CY), label * (2.0 * math.pi / cycle), jnp.float32)
        out_ref[pl.ds(0, 8), :] = jnp.cos(angle)
        out_ref[pl.ds(8, 8), :] = jnp.sin(angle)

    return pl.pallas_call(
        body,
        out_shape=jax.ShapeDtypeStruct((16, CY), jnp.float32),
        in_specs=[SMEM, HBM],
        out_specs=VMEM,
        scratch_shapes=[pltpu.SMEM(kpoint.shape, jnp.int32), pltpu.SemaphoreType.DMA],
        compiler_params=PARAMS,
        name="phase",
    )(place.reshape(1), kpoint)


def phase_rows(ref):
    return [jnp.concatenate([ref[pl.ds(8 * i, 1), :]] * CX, axis=1) for i in range(2)]


def ready_targets(targets, parts, planes, bands):
    count = len(targets)
    cells = count * planes * CELLS
    values = tile_values(bands)

    def body(*refs):
        ins, part_refs = refs[:count], refs[count : count + len(parts)]
        near_ref, weight_ref, sum_ref = refs[count + len(parts) :]
        total = part_refs[0][...]
        for ref in part_refs[1:]:
            total = total + ref[...]
        sum_ref[...] = total
        row = lax.broadcasted_iota(jnp.int32, (planes, CELLS), 0)

        def psi_at(d, b):
            return [ins[d % count][pl.ds((2 * b + c) * planes, planes), :] for c in range(2)]

        def above(d, b):
            here, next_slab = psi_at(d, b), psi_at(d + 1, b)
            return [
                jnp.where(row == planes - 1, pltpu.roll(n, planes - 1, 0), pltpu.roll(h, planes - 1, 0))
                for h, n in zip(here, next_slab)
            ]

        def below(d, b):
            here, last_slab = psi_at(d, b), psi_at(d - 1, b)
            return [jnp.where(row == 0, pltpu.roll(n, 1, 0), pltpu.roll(h, 1, 0)) for h, n in zip(here, last_slab)]

        for b in range(bands):
            here = psi_at(0, b)
            neighbours = (
                here,
                [swap_x(v) for v in here],
                [turn(v, 1) for v in here],
                [turn(v, -1) for v in here],
                above(0, b),
                below(0, b),
            )
            for n, pair in enumerate(neighbours):
                for c in range(2):
                    near_ref[pl.ds(((b * NEIGHBOURS + n) * 2 + c) * planes, planes), :] = pair[c]

        def put(d, q, i, value, scale):
            weight_ref[pl.ds(((d * len(values) + q) * FIELDS + i) * planes, planes), :] = value * scale

        def mixed(first, second, a, b, part):
            one = bond(*second[b], *first[a])
            if a == b:
                return 2.0 * one[0], -2.0 * one[1]
            two = bond(*second[a], *first[b])
            if part == 0:
                return one[0] + two[0], -(one[1] + two[1])
            return one[1] - two[1], one[0] - two[0]

        for d in range(count):
            here = [psi_at(d, b) for b in range(bands)]
            left = [[halves(v)[0] for v in pair] for pair in here]
            right = [[halves(v)[1] for v in pair] for pair in here]
            beside = [[turn(v, 1) for v in pair] for pair in here]
            over = [above(d, b) for b in range(bands)]
            for q, (a, b, part) in enumerate(values):
                put(d, q, 0, bond(*here[b], *here[a])[part], -1.0 / (DIAG * cells))
                scale = -1.0 / (DIAG * DIAG * cells)
                put(d, q, 1, jnp.concatenate(mixed(left, right, a, b, part), axis=1), 2.0 * scale)
                for i, other in ((2, beside), (4, over)):
                    for c, value in enumerate(mixed(here, other, a, b, part)):
                        put(d, q, i + c, value, scale)

    return pl.pallas_call(
        body,
        out_shape=(
            jax.ShapeDtypeStruct((bands * NEIGHBOURS * 2 * planes, CELLS), jnp.float32),
            jax.ShapeDtypeStruct((count * len(values) * FIELDS * planes, CELLS), jnp.float32),
            jax.ShapeDtypeStruct(parts[0].shape, jnp.float32),
        ),
        in_specs=[VMEM] * (count + len(parts)),
        out_specs=(VMEM, VMEM, VMEM),
        compiler_params=PARAMS,
        cost_estimate=pl.CostEstimate(flops=1000000000, bytes_accessed=0, transcendentals=0),
        name="ready_targets",
    )(*targets, *parts)


def tile_values(bands):
    return [(a, b, part) for a in range(bands) for b in range(a, bands) for part in range(2 if b > a else 1)]


def join(phase, own, packs, planes):
    count = len(packs)
    field_rows = FIELDS * planes

    def body(phase_ref, own_ref, *refs):
        ins, out = refs[:count], refs[count]
        cosine, sine = phase_rows(phase_ref)
        row = lax.broadcasted_iota(jnp.int32, (planes, CELLS), 0)

        def total(value):
            return jnp.sum(value, axis=0, keepdims=True)

        def end(ref, e):
            return [ref[pl.ds(SENT * planes + (2 * e + c) * BLOCK, BLOCK), :] for c in range(2)]

        def rebuilt(ref):
            held = [ref[pl.ds(i * planes, planes), :] for i in range(SENT)]
            last = held[0]
            for i in range(SENT - 1):
                last = jnp.where(row == 2 * i, pltpu.roll(held[i], 2 * i, 0), last)
                last = jnp.where(row == 2 * i + 1, pltpu.roll(held[i], (2 * i + 2 - planes) % planes, 0), last)
            for e, place in ((0, 0), (1, planes - 1)):
                re, im = end(ref, e)
                (re0, re1), (im0, im1) = halves(re), halves(im)
                values = (
                    re * re + im * im,
                    jnp.concatenate(bond(re0, im0, re1, im1), axis=1),
                    *bond(re, im, turn(re, 1), turn(im, 1)),
                )
                for i, value in enumerate(values):
                    held[i] = jnp.where(row == place, total(value), held[i])
            return held + [last]

        for d in range(count):
            here, there = ins[d], ins[(d + 1) % count]
            if d == 0:
                held = [own_ref[pl.ds(i * planes, planes), :] for i in range(FIELDS)]
            else:
                held = rebuilt(here)
            re, im = bond(*end(here, 1), *end(there, 0))
            re = jnp.where(row == planes - 1, total(re), held[4])
            im = jnp.where(row == planes - 1, total(im), held[5])
            held[4:] = [re * cosine + im * sine, im * cosine - re * sine]
            for i, field in enumerate(held):
                out[pl.ds(d * field_rows + i * planes, planes), :] = field

    return pl.pallas_call(
        body,
        out_shape=jax.ShapeDtypeStruct((count * field_rows, CELLS), jnp.float32),
        in_specs=[VMEM] * (2 + count),
        out_specs=VMEM,
        compiler_params=PARAMS,
        name="join_slabs",
    )(phase, own, *packs)


def apply(phase, parts, near, weights, planes, bands, count):
    field_rows = FIELDS * planes
    values = tile_values(bands)

    def body(phase_ref, *refs):
        part_refs, near_ref, weight_ref = refs[: len(parts)], refs[len(parts)], refs[len(parts) + 1]
        out_ref, tile_ref = refs[len(parts) + 2 :]
        cosine, sine = phase_rows(phase_ref)
        row = lax.broadcasted_iota(jnp.int32, (planes, CELLS), 0)

        def window(d, i):
            at = pl.ds(d * field_rows + i * planes, planes)
            total = part_refs[0][at, :]
            for ref in part_refs[1:]:
                total = total + ref[at, :]
            return total

        fields = []
        for d in range(count):
            held = [window(d, i) for i in range(FIELDS)]
            re, im = held[4:]
            fields.append(held[:4] + [re * cosine - im * sine, im * cosine + re * sine])

        dens, x_both, y_re, y_im, z_re, z_im = fields[0]
        dx_re, dx_im = halves(x_both)
        below = [
            jnp.where(row == 0, pltpu.roll(fields[count - 1][i], 1, 0), pltpu.roll(fields[0][i], 1, 0)) for i in (4, 5)
        ]
        factors = (
            (jnp.concatenate([dx_re, dx_re], axis=1) * 2.0, jnp.concatenate([dx_im, -dx_im], axis=1) * 2.0),
            (y_re, y_im),
            (turn(y_re, -1), -turn(y_im, -1)),
            (z_re, z_im),
            (below[0], -below[1]),
        )
        dens = dens * DIAG
        for b in range(bands):
            around = [
                [near_ref[pl.ds(((b * NEIGHBOURS + n) * 2 + c) * planes, planes), :] for c in range(2)]
                for n in range(NEIGHBOURS)
            ]
            acc_re = dens * around[0][0]
            acc_im = dens * around[0][1]
            for (wr, wi), (vr, vi) in zip(factors, around[1:]):
                acc_re = acc_re + (wr * vr - wi * vi)
                acc_im = acc_im + (wr * vi + wi * vr)
            out_ref[pl.ds(2 * b * planes, planes), :] = acc_re * (-1.0 / (DIAG * DIAG))
            out_ref[pl.ds((2 * b + 1) * planes, planes), :] = acc_im * (-1.0 / (DIAG * DIAG))

        found = {}
        for q, key in enumerate(values):
            total = jnp.zeros((planes, CELLS), jnp.float32)
            for d in range(count):
                for i in range(FIELDS):
                    at = pl.ds(((d * len(values) + q) * FIELDS + i) * planes, planes)
                    total = total + fields[d][i] * weight_ref[at, :]
            total = jnp.sum(total[:, :CY] + total[:, CY:], axis=0, keepdims=True)
            found[key] = jnp.sum(total, axis=1, keepdims=True)
        shape = (bands, 2)
        first = lax.broadcasted_iota(jnp.int32, shape, 0)
        second = lax.broadcasted_iota(jnp.int32, shape, 1)
        for a in range(bands):
            tile = jnp.zeros(shape, jnp.float32)
            for b in range(bands):
                low, high = min(a, b), max(a, b)
                tile = jnp.where((first == b) & (second == 0), found[low, high, 0], tile)
                if a != b:
                    imaginary = found[low, high, 1]
                    tile = jnp.where((first == b) & (second == 1), imaginary if a < b else -imaginary, tile)
            tile_ref[0, a] = tile

    return pl.pallas_call(
        body,
        out_shape=(
            jax.ShapeDtypeStruct((2 * bands * planes, CELLS), jnp.float32),
            jax.ShapeDtypeStruct((1, bands, bands, 2), jnp.float32),
        ),
        in_specs=[VMEM] * (len(parts) + 3),
        out_specs=(VMEM, VMEM),
        compiler_params=PARAMS,
        name="apply_window",
    )(phase, *parts, near, weights)


def shift(value, axis, distance):
    count = lax.axis_size(axis)
    return lax.ppermute(value, axis, [((i + distance) % count, i) for i in range(count)])


def body(targets, orbitals, block_index, occupied, kpoint):
    bands, planes = targets.shape[1], targets.shape[3]
    cycle, slabs = lax.axis_size("kring"), lax.axis_size("slab")
    place = lax.axis_index("kring")
    psi = targets.reshape(2 * bands * planes, CELLS)
    orb = orbitals.reshape(-1, planes, CX, CY).transpose(0, 2, 1, 3).reshape(-1, CY)

    phase = phase_of(kpoint, place, cycle)

    held = occupied.shape[1]
    words = occupied + 2 * lax.pad(block_index, jnp.int32(0), [(0, held - 1, 0)]).reshape(1, held)
    mask = (words & 1).astype(jnp.float32)
    own, pack = gather(block_index, spread(mask, diagonal(held)), orb, planes)
    packs = [pack] + [shift(pack, "slab", d) for d in range(1, slabs)]
    psis = [psi] + [shift(psi, "slab", d) for d in range(1, slabs)]
    mine = join(phase, own, packs, planes)

    left = shift(mine, "kring", -2)
    right = shift(mine, "kring", 2)
    odd = lax.rem(place, 2) == 1
    lacking = jnp.where(odd, left, right) + mine
    other = lax.ppermute(lacking, "kring", [(i, i ^ 1) for i in range(cycle)])
    held = ready_targets(psis, [mine, right, left], planes, bands)
    other, near, weights, total = lax.optimization_barrier((other, *held))
    exchange, tile = apply(phase, [total, other], near, weights, planes, bands, slabs)
    return exchange.reshape(targets.shape), tile


def solution(mesh):
    placed = (
        P("kring", None, None, "slab", None),
        P("kring", None, None, "slab", None),
        P("kring"),
        P("kring", None),
        P(),
    )
    return jax.shard_map(
        body,
        mesh=mesh,
        in_specs=placed,
        out_specs=(P("kring", None, None, "slab", None), P("kring", None, None, None)),
        check_vma=False,
    )
```

```python
import math

import jax
import jax.numpy as jnp
from jax import lax
from jax.experimental import pallas as pl
from jax.experimental.pallas import tpu as pltpu
from jax.sharding import PartitionSpec as P

CX = 2
CY = 128
CELLS = CX * CY
BLOCK = 16
FIELDS = 6
SENT = 5
NEIGHBOURS = 6
CHUNKS = 1
DIAG = 7.0

VMEM = pl.BlockSpec(memory_space=pltpu.VMEM)
SMEM = pl.BlockSpec(memory_space=pltpu.SMEM)
HBM = pl.BlockSpec(memory_space=pltpu.HBM)
PARAMS = pltpu.CompilerParams(vmem_limit_bytes=4 * 1024 * 1024)


def halves(field):
    return field[:, :CY], field[:, CY:]


def turn(field, shift):
    a, b = halves(field)
    amount = (-shift) % CY
    return jnp.concatenate([pltpu.roll(a, amount, 1), pltpu.roll(b, amount, 1)], axis=1)


def swap_x(field):
    a, b = halves(field)
    return jnp.concatenate([b, a], axis=1)


def bond(ar, ai, br, bi):
    return ar * br + ai * bi, ai * br - ar * bi


def gather_kernel(planes, index_ref, weight_ref, orb, own_ref, pack_ref):
    rows = 2 * CX * planes
    field_rows = SENT * planes
    first = index_ref[0] * BLOCK
    none = jnp.zeros((planes, CY), jnp.float32)
    dens, dy_re, dy_im, dz_re, dz_im = [[none] * CX for _ in range(5)]
    dx_re, dx_im = none, none
    for m in range(BLOCK):
        base = pl.multiple_of((first + m) * rows, 8)
        weight = weight_ref[pl.ds(first + m, 1), :]
        raw_re = [orb[pl.ds(base + x * planes, planes), :] for x in range(CX)]
        raw_im = [orb[pl.ds(base + (CX + x) * planes, planes), :] for x in range(CX)]
        re = [value * weight for value in raw_re]
        im = [value * weight for value in raw_im]
        part = bond(re[0], im[0], raw_re[1], raw_im[1])
        dx_re, dx_im = dx_re + part[0], dx_im + part[1]
        for x in range(CX):
            dens[x] = dens[x] + (re[x] * raw_re[x] + im[x] * raw_im[x])
            part = bond(re[x], im[x], pltpu.roll(raw_re[x], CY - 1, 1), pltpu.roll(raw_im[x], CY - 1, 1))
            dy_re[x], dy_im[x] = dy_re[x] + part[0], dy_im[x] + part[1]
            part = bond(re[x], im[x], pltpu.roll(raw_re[x], planes - 1, 0), pltpu.roll(raw_im[x], planes - 1, 0))
            dz_re[x], dz_im[x] = dz_re[x] + part[0], dz_im[x] + part[1]
    row = lax.broadcasted_iota(jnp.int32, (planes, CY), 0)
    for i, field in enumerate((dens, (dx_re, dx_im), dy_re, dy_im, dz_re, dz_im)):
        for x in range(CX):
            own_ref[pl.ds(i * planes, planes), pl.ds(x * CY, CY)] = field[x]
            if i == SENT:
                continue
            sent = field[x]
            if i < SENT - 1:
                low = pltpu.roll(dz_im[x], (-2 * i) % planes, 0)
                high = pltpu.roll(dz_im[x], (planes - 2 - 2 * i) % planes, 0)
                sent = jnp.where(row == 0, low, jnp.where(row == planes - 1, high, sent))
            pack_ref[pl.ds(i * planes, planes), pl.ds(x * CY, CY)] = sent
    column = weight_ref[pl.ds(pl.multiple_of(first, BLOCK), BLOCK), :]
    for e, plane in enumerate((0, planes - 1)):
        for c in range(2):
            for x in range(CX):
                ends = orb[pl.ds(first * rows + (c * CX + x) * planes + plane, BLOCK, stride=rows), :] * column
                pack_ref[pl.ds(field_rows + (2 * e + c) * BLOCK, BLOCK), pl.ds(x * CY, CY)] = ends


def diagonal(count):
    def body(out):
        row = lax.broadcasted_iota(jnp.int32, (count, count), 0)
        column = lax.broadcasted_iota(jnp.int32, (count, count), 1)
        out[...] = jnp.where(row == column, 1.0, 0.0)

    return pl.pallas_call(
        body,
        out_shape=jax.ShapeDtypeStruct((count, count), jnp.float32),
        out_specs=VMEM,
        compiler_params=PARAMS,
        cost_estimate=pl.CostEstimate(flops=1000000000, bytes_accessed=0, transcendentals=0),
        name="diagonal",
    )()


def spread(mask, ones):
    count = mask.shape[1]

    def body(mask_ref, ones_ref, out):
        held = jnp.sum(mask_ref[...] * ones_ref[...], axis=1, keepdims=True)
        out[...] = jnp.broadcast_to(held, (count, CY))

    return pl.pallas_call(
        body,
        out_shape=jax.ShapeDtypeStruct((count, CY), jnp.float32),
        in_specs=[VMEM, VMEM],
        out_specs=VMEM,
        compiler_params=PARAMS,
        name="spread_mask",
    )(mask, ones)


def gather(block_index, weights, orb, planes):
    def body(*refs):
        gather_kernel(planes, *refs)

    return pl.pallas_call(
        body,
        out_shape=(
            jax.ShapeDtypeStruct((FIELDS * planes, CELLS), jnp.float32),
            jax.ShapeDtypeStruct((SENT * planes + 4 * BLOCK, CELLS), jnp.float32),
        ),
        in_specs=[SMEM, VMEM, VMEM],
        out_specs=(VMEM, VMEM),
        compiler_params=PARAMS,
        name="local_fields",
    )(block_index, weights, orb)


def phase_of(kpoint, place, cycle, targets):
    def body(place_ref, kpoint_hbm, targets_ref, out_ref, held_ref, labels, sem):
        load = pltpu.make_async_copy(kpoint_hbm, labels, sem)
        load.start()
        held_ref[...] = targets_ref[...]
        load.wait()
        label = labels[place_ref[0]].astype(jnp.float32)
        angle = jnp.full((8, CY), label * (2.0 * math.pi / cycle), jnp.float32)
        out_ref[pl.ds(0, 8), :] = jnp.cos(angle)
        out_ref[pl.ds(8, 8), :] = jnp.sin(angle)

    return pl.pallas_call(
        body,
        out_shape=(
            jax.ShapeDtypeStruct((16, CY), jnp.float32),
            jax.ShapeDtypeStruct(targets.shape, jnp.float32),
        ),
        in_specs=[SMEM, HBM, VMEM],
        out_specs=(VMEM, VMEM),
        scratch_shapes=[pltpu.SMEM(kpoint.shape, jnp.int32), pltpu.SemaphoreType.DMA],
        compiler_params=PARAMS,
        name="phase",
    )(place.reshape(1), kpoint, targets)


def phase_rows(ref):
    return [jnp.concatenate([ref[pl.ds(8 * i, 1), :]] * CX, axis=1) for i in range(2)]


def ready_targets(targets, parts, planes, bands):
    count = len(targets)
    cells = count * planes * CELLS
    values = tile_values(bands)

    def body(*refs):
        ins, part_refs = refs[:count], refs[count : count + len(parts)]
        near_ref, weight_ref, sum_ref = refs[count + len(parts) :]
        total = part_refs[0][...]
        for ref in part_refs[1:]:
            total = total + ref[...]
        sum_ref[...] = total
        row = lax.broadcasted_iota(jnp.int32, (planes, CELLS), 0)

        def psi_at(d, b):
            return [ins[d % count][pl.ds((2 * b + c) * planes, planes), :] for c in range(2)]

        def above(d, b):
            here, next_slab = psi_at(d, b), psi_at(d + 1, b)
            return [
                jnp.where(row == planes - 1, pltpu.roll(n, planes - 1, 0), pltpu.roll(h, planes - 1, 0))
                for h, n in zip(here, next_slab)
            ]

        def below(d, b):
            here, last_slab = psi_at(d, b), psi_at(d - 1, b)
            return [jnp.where(row == 0, pltpu.roll(n, 1, 0), pltpu.roll(h, 1, 0)) for h, n in zip(here, last_slab)]

        for b in range(bands):
            here = psi_at(0, b)
            neighbours = (
                here,
                [swap_x(v) for v in here],
                [turn(v, 1) for v in here],
                [turn(v, -1) for v in here],
                above(0, b),
                below(0, b),
            )
            for n, pair in enumerate(neighbours):
                for c in range(2):
                    near_ref[pl.ds(((b * NEIGHBOURS + n) * 2 + c) * planes, planes), :] = pair[c]

        def put(d, q, i, value, scale):
            weight_ref[pl.ds(((d * len(values) + q) * FIELDS + i) * planes, planes), :] = value * scale

        def mixed(first, second, a, b, part):
            one = bond(*second[b], *first[a])
            if a == b:
                return 2.0 * one[0], -2.0 * one[1]
            two = bond(*second[a], *first[b])
            if part == 0:
                return one[0] + two[0], -(one[1] + two[1])
            return one[1] - two[1], one[0] - two[0]

        for d in range(count):
            here = [psi_at(d, b) for b in range(bands)]
            left = [[halves(v)[0] for v in pair] for pair in here]
            right = [[halves(v)[1] for v in pair] for pair in here]
            beside = [[turn(v, 1) for v in pair] for pair in here]
            over = [above(d, b) for b in range(bands)]
            for q, (a, b, part) in enumerate(values):
                put(d, q, 0, bond(*here[b], *here[a])[part], -1.0 / (DIAG * cells))
                scale = -1.0 / (DIAG * DIAG * cells)
                put(d, q, 1, jnp.concatenate(mixed(left, right, a, b, part), axis=1), 2.0 * scale)
                for i, other in ((2, beside), (4, over)):
                    for c, value in enumerate(mixed(here, other, a, b, part)):
                        put(d, q, i + c, value, scale)

    return pl.pallas_call(
        body,
        out_shape=(
            jax.ShapeDtypeStruct((bands * NEIGHBOURS * 2 * planes, CELLS), jnp.float32),
            jax.ShapeDtypeStruct((count * len(values) * FIELDS * planes, CELLS), jnp.float32),
            jax.ShapeDtypeStruct(parts[0].shape, jnp.float32),
        ),
        in_specs=[VMEM] * (count + len(parts)),
        out_specs=(VMEM, VMEM, VMEM),
        compiler_params=PARAMS,
        cost_estimate=pl.CostEstimate(flops=1000000000, bytes_accessed=0, transcendentals=0),
        name="ready_targets",
    )(*targets, *parts)


def tile_values(bands):
    return [(a, b, part) for a in range(bands) for b in range(a, bands) for part in range(2 if b > a else 1)]


def join(phase, own, packs, planes):
    count = len(packs)
    field_rows = FIELDS * planes

    def body(phase_ref, own_ref, *refs):
        ins, out = refs[:count], refs[count]
        cosine, sine = phase_rows(phase_ref)
        row = lax.broadcasted_iota(jnp.int32, (planes, CELLS), 0)

        def total(value):
            return jnp.sum(value, axis=0, keepdims=True)

        def end(ref, e):
            return [ref[pl.ds(SENT * planes + (2 * e + c) * BLOCK, BLOCK), :] for c in range(2)]

        def rebuilt(ref):
            held = [ref[pl.ds(i * planes, planes), :] for i in range(SENT)]
            last = held[0]
            for i in range(SENT - 1):
                last = jnp.where(row == 2 * i, pltpu.roll(held[i], 2 * i, 0), last)
                last = jnp.where(row == 2 * i + 1, pltpu.roll(held[i], (2 * i + 2 - planes) % planes, 0), last)
            for e, place in ((0, 0), (1, planes - 1)):
                re, im = end(ref, e)
                (re0, re1), (im0, im1) = halves(re), halves(im)
                values = (
                    re * re + im * im,
                    jnp.concatenate(bond(re0, im0, re1, im1), axis=1),
                    *bond(re, im, turn(re, 1), turn(im, 1)),
                )
                for i, value in enumerate(values):
                    held[i] = jnp.where(row == place, total(value), held[i])
            return held + [last]

        for d in range(count):
            here, there = ins[d], ins[(d + 1) % count]
            if d == 0:
                held = [own_ref[pl.ds(i * planes, planes), :] for i in range(FIELDS)]
            else:
                held = rebuilt(here)
            re, im = bond(*end(here, 1), *end(there, 0))
            re = jnp.where(row == planes - 1, total(re), held[4])
            im = jnp.where(row == planes - 1, total(im), held[5])
            held[4:] = [re * cosine + im * sine, im * cosine - re * sine]
            for i, field in enumerate(held):
                out[pl.ds(d * field_rows + i * planes, planes), :] = field

    return pl.pallas_call(
        body,
        out_shape=jax.ShapeDtypeStruct((count * field_rows, CELLS), jnp.float32),
        in_specs=[VMEM] * (2 + count),
        out_specs=VMEM,
        compiler_params=PARAMS,
        name="join_slabs",
    )(phase, own, *packs)


def apply(phase, parts, near, weights, planes, bands, count):
    field_rows = FIELDS * planes
    values = tile_values(bands)

    def body(phase_ref, *refs):
        part_refs, near_ref, weight_ref = refs[: len(parts)], refs[len(parts)], refs[len(parts) + 1]
        out_ref, tile_ref = refs[len(parts) + 2 :]
        cosine, sine = phase_rows(phase_ref)
        row = lax.broadcasted_iota(jnp.int32, (planes, CELLS), 0)

        def window(d, i):
            at = pl.ds(d * field_rows + i * planes, planes)
            total = part_refs[0][at, :]
            for ref in part_refs[1:]:
                total = total + ref[at, :]
            return total

        fields = []
        for d in range(count):
            held = [window(d, i) for i in range(FIELDS)]
            re, im = held[4:]
            fields.append(held[:4] + [re * cosine - im * sine, im * cosine + re * sine])

        dens, x_both, y_re, y_im, z_re, z_im = fields[0]
        dx_re, dx_im = halves(x_both)
        below = [
            jnp.where(row == 0, pltpu.roll(fields[count - 1][i], 1, 0), pltpu.roll(fields[0][i], 1, 0)) for i in (4, 5)
        ]
        factors = (
            (jnp.concatenate([dx_re, dx_re], axis=1) * 2.0, jnp.concatenate([dx_im, -dx_im], axis=1) * 2.0),
            (y_re, y_im),
            (turn(y_re, -1), -turn(y_im, -1)),
            (z_re, z_im),
            (below[0], -below[1]),
        )
        dens = dens * DIAG
        for b in range(bands):
            around = [
                [near_ref[pl.ds(((b * NEIGHBOURS + n) * 2 + c) * planes, planes), :] for c in range(2)]
                for n in range(NEIGHBOURS)
            ]
            acc_re = dens * around[0][0]
            acc_im = dens * around[0][1]
            for (wr, wi), (vr, vi) in zip(factors, around[1:]):
                acc_re = acc_re + (wr * vr - wi * vi)
                acc_im = acc_im + (wr * vi + wi * vr)
            out_ref[pl.ds(2 * b * planes, planes), :] = acc_re * (-1.0 / (DIAG * DIAG))
            out_ref[pl.ds((2 * b + 1) * planes, planes), :] = acc_im * (-1.0 / (DIAG * DIAG))

        found = {}
        for q, key in enumerate(values):
            total = jnp.zeros((planes, CELLS), jnp.float32)
            for d in range(count):
                for i in range(FIELDS):
                    at = pl.ds(((d * len(values) + q) * FIELDS + i) * planes, planes)
                    total = total + fields[d][i] * weight_ref[at, :]
            total = jnp.sum(total[:, :CY] + total[:, CY:], axis=0, keepdims=True)
            found[key] = jnp.sum(total, axis=1, keepdims=True)
        shape = (bands, 2)
        first = lax.broadcasted_iota(jnp.int32, shape, 0)
        second = lax.broadcasted_iota(jnp.int32, shape, 1)
        for a in range(bands):
            tile = jnp.zeros(shape, jnp.float32)
            for b in range(bands):
                low, high = min(a, b), max(a, b)
                tile = jnp.where((first == b) & (second == 0), found[low, high, 0], tile)
                if a != b:
                    imaginary = found[low, high, 1]
                    tile = jnp.where((first == b) & (second == 1), imaginary if a < b else -imaginary, tile)
            tile_ref[0, a] = tile

    return pl.pallas_call(
        body,
        out_shape=(
            jax.ShapeDtypeStruct((2 * bands * planes, CELLS), jnp.float32),
            jax.ShapeDtypeStruct((1, bands, bands, 2), jnp.float32),
        ),
        in_specs=[VMEM] * (len(parts) + 3),
        out_specs=(VMEM, VMEM),
        compiler_params=PARAMS,
        name="apply_window",
    )(phase, *parts, near, weights)


def shift(value, axis, distance):
    count = lax.axis_size(axis)
    return lax.ppermute(value, axis, [((i + distance) % count, i) for i in range(count)])


def body(targets, orbitals, block_index, occupied, kpoint):
    bands, planes = targets.shape[1], targets.shape[3]
    cycle, slabs = lax.axis_size("kring"), lax.axis_size("slab")
    place = lax.axis_index("kring")
    psi = targets.reshape(2 * bands * planes, CELLS)
    orb = orbitals.reshape(-1, planes, CX, CY).transpose(0, 2, 1, 3).reshape(-1, CY)

    phase, psi = phase_of(kpoint, place, cycle, psi)

    held = occupied.shape[1]
    words = occupied + 2 * lax.pad(block_index, jnp.int32(0), [(0, held - 1, 0)]).reshape(1, held)
    mask = (words & 1).astype(jnp.float32)
    own, pack = gather(block_index, spread(mask, diagonal(held)), orb, planes)
    packs = [pack] + [shift(pack, "slab", d) for d in range(1, slabs)]
    psis = [psi] + [shift(psi, "slab", d) for d in range(1, slabs)]
    mine = join(phase, own, packs, planes)

    left = shift(mine, "kring", -2)
    right = shift(mine, "kring", 2)
    held = ready_targets(psis, [mine], planes, bands)
    right, left, near, weights, total = lax.optimization_barrier((right, left, *held))
    odd = lax.rem(place, 2) == 1
    lacking = jnp.where(odd, left, right) + mine
    other = lax.ppermute(lacking, "kring", [(i, i ^ 1) for i in range(cycle)])
    exchange, tile = apply(phase, [total, right, left, other], near, weights, planes, bands, slabs)
    return exchange.reshape(targets.shape), tile


def solution(mesh):
    placed = (
        P("kring", None, None, "slab", None),
        P("kring", None, None, "slab", None),
        P("kring"),
        P("kring", None),
        P(),
    )
    return jax.shard_map(
        body,
        mesh=mesh,
        in_specs=placed,
        out_specs=(P("kring", None, None, "slab", None), P("kring", None, None, None)),
        check_vma=False,
    )
```
